128 devices in a mesh: dp: 8 (over z, x_hi), chan: 16 (over x_lo, y, core).
Axes of the slice: x: 4 (x_hi: 2, x_lo: 2; x = x_hi * 2 + x_lo), y: 4, z: 4, core: 2. Of those that a mesh axis runs over, the one named last changes fastest.
Arguments:
- tokens: bfloat16 [8192, 8192], P('dp', 'chan'), may hold values from -6 to 6
- first_up: bfloat16 [32, 256, 256], P('chan'), may hold values from -0.375 to 0.375
- second_up: bfloat16 [32, 256, 1024], P('chan'), may hold values from -0.375 to 0.375
- first_down: bfloat16 [32, 1024, 256], P('chan'), may hold values from -0.1875 to 0.1875
- second_down: bfloat16 [32, 256, 256], P('chan'), may hold values from -0.375 to 0.375
- perm_up: int32 [8192], replicated, may hold values from 0 to 8191, as said below
- perm_down: int32 [8192], replicated, may hold values from 0 to 8191, as said below
- cotangent: bfloat16 [8192, 8192], P('dp', 'chan'), may hold values from -6 to 6
Outputs:
- mixed: bfloat16 [8192, 8192], P('dp', 'chan')
- input_grad: bfloat16 [8192, 8192], P('dp', 'chan')
- grad_first_up: float32 [32, 256, 256], P('chan')
- grad_second_up: float32 [32, 256, 1024], P('chan')
- grad_first_down: float32 [32, 1024, 256], P('chan')
- grad_second_down: float32 [32, 256, 256], P('chan')
The draws below stay inside these ranges and needn't reach their ends.
Inputs may be any that keep to these rules, and one draw needn't show every extreme that they name: `perm_up`: A permutation of the channels; of the outputs j in one aligned group of 512 channels, exactly 32 take their source from each aligned group of 512 channels. `perm_down`: as perm_up, drawn independently.
All inputs are finite; a program needn't handle non-finite values.
Results may differ from the reference program's by a relative error of at most 0.007.
Values may be sent and summed in bfloat16 or wider, within the bound.
No kernel may reach another device: no remote copies, remote signals or barrier semaphores. Data moves between devices by JAX's collectives and lax.ppermute only.
A program may use at most 128 MiB of HBM per device.

```python
import jax
import jax.numpy as jnp
from jax import lax

D = 8192
BLK = 256
TOK_DEV = 1024
NBLK = 32
HB = 1024
CHAN_DEV = 512
TOKENS = 8192
N_DP = 8


def balanced_routing(key):
    group_count = D // CHAN_DEV
    per_peer = CHAN_DEV // group_count
    key_source, key_order = jax.random.split(key)
    own_shuffle = jax.vmap(lambda subkey: jax.random.permutation(subkey, CHAN_DEV))(jax.random.split(key_source, group_count))
    sources = own_shuffle.astype(jnp.int32) + (jnp.arange(group_count, dtype=jnp.int32) * CHAN_DEV)[:, None]
    arranged = sources.reshape(group_count, group_count, per_peer).transpose(1, 0, 2).reshape(group_count, CHAN_DEV)
    dest_shuffle = jax.vmap(lambda subkey: jax.random.permutation(subkey, CHAN_DEV))(jax.random.split(key_order, group_count))
    return jnp.take_along_axis(arranged, dest_shuffle.astype(jnp.int32), axis=1).reshape(D).astype(jnp.int32)


def draw_perm_up(key, part):
    key = jax.random.fold_in(key, 11)
    return balanced_routing(key)


def draw_perm_down(key, part):
    key = jax.random.fold_in(key, 23)
    return balanced_routing(key)


def level_of(own_key, extent, cuts, low, top_value):
    level = 1.0
    for axis_at, parts in cuts:
        heights = jax.random.uniform(jax.random.fold_in(jax.random.fold_in(own_key, 6), axis_at), (parts,), jnp.float32, low / len(cuts), top_value / len(cuts))
        level = level * jnp.repeat(jnp.exp(heights), extent[axis_at] // parts).reshape((-1,) + (1,) * (len(extent) - 1 - axis_at))
    return level


def centred(stream_key, dims, width, most, cuts=(), held_as=jnp.bfloat16):
    drawn = width * jax.random.normal(stream_key, dims, jnp.float32)
    if cuts:
        drawn = drawn * level_of(stream_key, dims, cuts, -0.22, 0.18)
    return jnp.clip(drawn, -most, most).astype(held_as)


def setup_inputs(seed: int = 0) -> dict:
    keys = jax.random.split(jax.random.key(seed), 9)
    tokens = centred(keys[0], (TOKENS, D), 1.0, 6.0, ((0, 8), (1, 16)))
    first_up = centred(keys[1], (NBLK, BLK, BLK), BLK ** -0.5, 0.375, ((0, 16),))
    second_up = centred(keys[2], (NBLK, BLK, HB), BLK ** -0.5, 0.375, ((0, 16),))
    first_down = centred(keys[3], (NBLK, HB, BLK), HB ** -0.5, 0.1875, ((0, 16),))
    second_down = centred(keys[4], (NBLK, BLK, BLK), BLK ** -0.5, 0.375, ((0, 16),))
    perm_up = draw_perm_up(jax.random.fold_in(keys[8], 71), 0)
    perm_down = draw_perm_down(jax.random.fold_in(keys[8], 71), 0)
    cotangent = centred(keys[7], (TOKENS, D), 1.0, 6.0, ((0, 8), (1, 16)))
    return {"tokens": tokens, "first_up": first_up, "second_up": second_up, "first_down": first_down, "second_down": second_down, "perm_up": perm_up, "perm_down": perm_down, "cotangent": cotangent}


def gelu_tanh(inputs):
    return jax.nn.gelu(inputs, approximate=True)

def block_apply(inputs, weight):
    row_count = inputs.shape[0]
    blocks = weight.shape[0]
    pieces = inputs.reshape(row_count, blocks, weight.shape[1]).astype(jnp.float32)
    result = jnp.einsum('rki,kio->rko', pieces, weight.astype(jnp.float32))
    return result.reshape(row_count, blocks * weight.shape[2])

def block_back(grads, weight):
    row_count = grads.shape[0]
    blocks = weight.shape[0]
    pieces = grads.reshape(row_count, blocks, weight.shape[2]).astype(jnp.float32)
    result = jnp.einsum('rko,kio->rki', pieces, weight.astype(jnp.float32))
    return result.reshape(row_count, blocks * weight.shape[1])

def block_grad(inputs, grads, weight):
    row_count = inputs.shape[0]
    blocks = weight.shape[0]
    left = inputs.reshape(row_count, blocks, weight.shape[1]).astype(jnp.float32)
    right = grads.reshape(row_count, blocks, weight.shape[2]).astype(jnp.float32)
    return jnp.einsum('rki,rko->kio', left, right)

def reference(tokens, first_up, second_up, first_down, second_down, perm_up, perm_down, cotangent):
    undo_up = jnp.argsort(perm_up).astype(jnp.int32)
    undo_down = jnp.argsort(perm_down).astype(jnp.int32)

    def one_block(totals, inputs_pair):
        tok_block, cot_block = inputs_pair
        first_act = block_apply(tok_block, first_up).astype(jnp.bfloat16)
        mixed_in = first_act[:, perm_up]
        hidden = block_apply(mixed_in, second_up)
        activated, gelu_back = jax.vjp(gelu_tanh, hidden)
        act_low = activated.astype(jnp.bfloat16)
        narrowed = block_apply(act_low, first_down).astype(jnp.bfloat16)
        routed = narrowed[:, perm_down]
        mixed = block_apply(routed, second_down).astype(jnp.bfloat16)
        g_sd = block_grad(routed, cot_block, second_down)
        routed_grad = block_back(cot_block, second_down).astype(jnp.bfloat16)
        narrowed_grad = routed_grad[:, undo_down]
        g_fd = block_grad(act_low, narrowed_grad, first_down)
        act_grad = block_back(narrowed_grad, first_down)
        hidden_grad = gelu_back(act_grad)[0].astype(jnp.bfloat16)
        g_su = block_grad(mixed_in, hidden_grad, second_up)
        mixed_grad = block_back(hidden_grad, second_up).astype(jnp.bfloat16)
        first_grad = mixed_grad[:, undo_up]
        g_fu = block_grad(tok_block, first_grad, first_up)
        input_grad = block_back(first_grad, first_up).astype(jnp.bfloat16)
        new_totals = (totals[0] + g_fu, totals[1] + g_su, totals[2] + g_fd, totals[3] + g_sd)
        return (new_totals, (mixed, input_grad))
    zeros_init = (jnp.zeros(first_up.shape, jnp.float32), jnp.zeros(second_up.shape, jnp.float32), jnp.zeros(first_down.shape, jnp.float32), jnp.zeros(second_down.shape, jnp.float32))
    tok_blocks = tokens.reshape(N_DP, TOK_DEV, D)
    cot_blocks = cotangent.reshape(N_DP, TOK_DEV, D)
    totals, outputs = lax.scan(one_block, zeros_init, (tok_blocks, cot_blocks))
    mixed = outputs[0].reshape(TOKENS, D)
    input_grad = outputs[1].reshape(TOKENS, D)
    return (mixed, input_grad, totals[0], totals[1], totals[2], totals[3])
```

```python
import jax
import jax.numpy as jnp
from jax import lax
from jax.experimental import pallas as pl
from jax.experimental.pallas import tpu as pltpu
from jax.sharding import PartitionSpec as P

BF = jnp.bfloat16
F32 = jnp.float32
GELU_C = 0.7978845608028654
GELU_A = 0.044715
VMEM_BYTES = 56 * 2**20


def nn(left, right):
    return lax.dot_general(left, right, (((1,), (0,)), ((), ())), preferred_element_type=F32)


def nt(left, right):
    return lax.dot_general(left, right, (((1,), (1,)), ((), ())), preferred_element_type=F32)


def tn(left, right):
    return lax.dot_general(left, right, (((0,), (0,)), ((), ())), preferred_element_type=F32)


def one_hots(perm_ref, me, before, source_ref, target_ref):
    perm = perm_ref[...]
    slot = lax.broadcasted_iota(jnp.int32, (32, 512), 0).astype(F32)
    lane = lax.broadcasted_iota(jnp.int32, (32, 512), 1).astype(F32)
    group = lax.shift_right_logical(perm, 9)
    mine = group == me
    rank = nn(jnp.where(mine, 1.0, 0.0).astype(BF), before)
    rank = jnp.where(mine, rank, -1.0)
    local = (perm & 511).astype(F32)
    for r in range(16):
        hit = rank[r : r + 1, :] == slot
        channel = jnp.sum(jnp.where(hit, local[r : r + 1, :], 0.0), axis=1, keepdims=True)
        source_ref[32 * r : 32 * r + 32, :] = jnp.where(channel == lane, 1.0, 0.0).astype(BF)
    row = lax.shift_right_logical(perm_ref[pl.ds(me, 1), :], 9)
    from_group = row == lax.broadcasted_iota(jnp.int32, (16, 512), 0)
    rank = nn(jnp.where(from_group, 1.0, 0.0).astype(BF), before)
    rank = jnp.where(from_group, rank, -1.0)
    for s in range(16):
        target_ref[32 * s : 32 * s + 32, :] = jnp.where(rank[s : s + 1, :] == slot, 1.0, 0.0).astype(BF)


def stage_one(tok_ref, cot_ref, fu_ref, sd_ref, pu_ref, pd_ref, out_ref, su_ref, tu_ref, sdn_ref, tdn_ref, wu_ref, wd_ref):
    me = lax.axis_index("chan")
    before = jnp.where(
        lax.broadcasted_iota(jnp.int32, (512, 512), 0) < lax.broadcasted_iota(jnp.int32, (512, 512), 1), 1.0, 0.0
    ).astype(BF)
    one_hots(pu_ref, me, before, su_ref, tu_ref)
    one_hots(pd_ref, me, before, sdn_ref, tdn_ref)
    for k in range(2):
        cols = slice(256 * k, 256 * k + 256)
        wu_ref[:, cols] = nt(su_ref[:, cols], fu_ref[k]).astype(BF)
        wd_ref[:, cols] = nn(tdn_ref[:, cols], sd_ref[k]).astype(BF)
    out_ref[:, 0:32, :] = nt(wu_ref[...], tok_ref[...]).astype(BF).reshape(16, 32, 1024)
    out_ref[:, 32:64, :] = nt(wd_ref[...], cot_ref[...]).astype(BF).reshape(16, 32, 1024)


def stage_two(r_ref, tu_ref, sdn_ref, su_ref, fd_ref, out_ref, g0, g1, g2, g3, act, hg, nar, mix, parts, sems):
    mixed_in = tn(tu_ref[...], r_ref[:, 0:32, :].reshape(512, 1024)).astype(BF)
    nar_grad = tn(sdn_ref[...], r_ref[:, 32:64, :].reshape(512, 1024)).astype(BF)
    for k in range(2):
        mi = mixed_in[256 * k : 256 * k + 256, :]
        ng = nar_grad[256 * k : 256 * k + 256, :]
        for c in range(4):
            units = slice(256 * c, 256 * c + 256)
            v = tn(su_ref[k, :, units], mi)
            up = nn(fd_ref[k, units, :], ng)
            sq = v * v
            h = 0.5 + 0.5 * jnp.tanh(v * (GELU_C + (GELU_C * GELU_A) * sq))
            a = (v * h).astype(BF)
            d = v * ((2 * GELU_C) + (6 * GELU_C * GELU_A) * sq)
            b = (up * (h * (1.0 + (1.0 - h) * d))).astype(BF)
            act[units, :] = a
            hg[units, :] = b
            gsu = nt(mi, b).astype(BF)
            gfd = nt(a, ng).astype(BF)
            for i in range(2):
                rows = slice(128 * i, 128 * i + 128)
                parts[2 * k + i, 0:128, units] = gsu[rows, :]
                at = (c % 2) * 512 + 256 * i
                parts[2 * k + c // 2, 128:256, at : at + 256] = gfd[rows, :]
        nar[256 * k : 256 * k + 256, :] = tn(fd_ref[k], act[...]).astype(BF)
        mix[256 * k : 256 * k + 256, :] = nn(su_ref[k], hg[...]).astype(BF)
    z = lax.shift_right_logical(lax.axis_index("dp"), 1)
    copies = [
        pltpu.make_async_copy(parts.at[(z + i) & 3], g, sems.at[i]) for i, g in enumerate((g0, g1, g2, g3))
    ]
    for copy in copies:
        copy.start()
    out_ref[:, 0:32, :] = nn(sdn_ref[...], nar[...]).astype(BF).reshape(16, 32, 1024)
    out_ref[:, 32:64, :] = nn(tu_ref[...], mix[...]).astype(BF).reshape(16, 32, 1024)
    for copy in copies:
        copy.wait()


def stage_three(r_ref, tok_ref, cot_ref, su_ref, tdn_ref, wu_ref, wd_ref, mixed_ref, ig_ref, t_ref):
    rc = r_ref[:, 0:32, :].reshape(512, 1024)
    rd = r_ref[:, 32:64, :].reshape(512, 1024)
    sd_slots = nn(rc, cot_ref[...]).astype(BF)
    fu_slots = nn(rd, tok_ref[...]).astype(BF)
    for k in range(2):
        cols = slice(256 * k, 256 * k + 256)
        gsd = tn(tdn_ref[:, cols], sd_slots[:, cols]).astype(BF)
        gfu = tn(fu_slots[:, cols], su_ref[:, cols]).astype(BF)
        for i in range(4):
            rows = slice(64 * i, 64 * i + 64)
            t_ref[4 * k + i, :, 0:256] = gsd[rows, :]
            t_ref[4 * k + i, :, 256:512] = gfu[rows, :]
    mixed_ref[...] = tn(rc, wd_ref[...]).astype(BF)
    ig_ref[...] = tn(rd, wu_ref[...]).astype(BF)


def finish(f0, f1, f2, f3, t_ref, gfu_ref, gsu_ref, gfd_ref, gsd_ref, parts, sems):
    z = lax.shift_right_logical(lax.axis_index("dp"), 1)
    copies = [
        pltpu.make_async_copy(f, parts.at[(z - i) & 3], sems.at[i]) for i, f in enumerate((f0, f1, f2, f3))
    ]
    for copy in copies:
        copy.start()
    for k in range(2):
        for i in range(4):
            rows = slice(64 * i, 64 * i + 64)
            gsd_ref[k, rows, :] = t_ref[4 * k + i, :, 0:256].astype(F32)
            gfu_ref[k, rows, :] = t_ref[4 * k + i, :, 256:512].astype(F32)
    for copy in copies:
        copy.wait()
    for c in range(4):
        k, half = c // 2, c % 2
        gsu_ref[k, 128 * half : 128 * half + 128, :] = parts[c, 0:128, :].astype(F32)
        for b in range(4):
            at = 512 * half + 128 * b
            gfd_ref[k, at : at + 128, :] = parts[c, 128:256, 256 * b : 256 * b + 256].astype(F32)


def like(*shape, dtype=BF):
    return jax.ShapeDtypeStruct(shape, dtype)


def whole(count):
    return [pl.BlockSpec(memory_space=pltpu.VMEM)] * count


def placed_anywhere(count):
    return [pl.BlockSpec(memory_space=pl.ANY)] * count


PARAMS = pltpu.CompilerParams(vmem_limit_bytes=VMEM_BYTES)


def shift_z(step):
    return [(2 * z + x, 2 * ((z + step) % 4) + x) for z in range(4) for x in range(2)]


SWAP_X = [(2 * z + x, 2 * z + 1 - x) for z in range(4) for x in range(2)]


def exchange(values, axis):
    return lax.all_to_all(values, axis, split_axis=0, concat_axis=0, tiled=True)


def per_device(tokens, first_up, second_up, first_down, second_down, perm_up, perm_down, cotangent):
    square = like(512, 512)
    sent, up_src, up_tgt, down_src, down_tgt, w_up, w_down = pl.pallas_call(
        stage_one,
        out_shape=(like(16, 64, 1024),) + (square,) * 6,
        in_specs=whole(6),
        out_specs=whole(7),
        compiler_params=PARAMS,
        name="stage_one",
    )(tokens, cotangent, first_up, second_down, perm_up.reshape(16, 512), perm_down.reshape(16, 512))
    got = exchange(sent, "chan")
    part = like(256, 1024)
    sent, g0, g1, g2, g3 = pl.pallas_call(
        stage_two,
        out_shape=(like(16, 64, 1024), part, part, part, part),
        in_specs=whole(5),
        out_specs=whole(1) + placed_anywhere(4),
        scratch_shapes=[
            pltpu.VMEM((1024, 1024), BF),
            pltpu.VMEM((1024, 1024), BF),
            pltpu.VMEM((512, 1024), BF),
            pltpu.VMEM((512, 1024), BF),
            pltpu.VMEM((4, 256, 1024), BF),
            pltpu.SemaphoreType.DMA((4,)),
        ],
        compiler_params=PARAMS,
        name="stage_two",
    )(got, up_tgt, down_src, second_up, first_down)
    near = [lax.ppermute(g, "dp", shift_z(i + 1)) for i, g in enumerate((g1, g2, g3))]
    got = exchange(sent, "chan")
    mixed, input_grad, tail = pl.pallas_call(
        stage_three,
        out_shape=(like(1024, 512), like(1024, 512), like(8, 64, 512)),
        in_specs=whole(7),
        out_specs=whole(3),
        compiler_params=PARAMS,
        name="stage_three",
    )(got, tokens, cotangent, up_src, down_tgt, w_up, w_down)
    mine = (g0.astype(F32) + near[0].astype(F32) + near[1].astype(F32) + near[2].astype(F32)).astype(BF)
    other = lax.ppermute(mine, "dp", SWAP_X)
    f0 = (mine.astype(F32) + other.astype(F32)).astype(BF)
    far = [lax.ppermute(f0, "dp", shift_z(i)) for i in (1, 2, 3)]
    tail = exchange(tail, "dp")
    tail = jnp.sum(tail.astype(F32), axis=0).astype(BF)
    tail = exchange(jnp.broadcast_to(tail[None], (8, 64, 512)), "dp")
    grad_fu, grad_su, grad_fd, grad_sd = pl.pallas_call(
        finish,
        out_shape=(
            like(2, 256, 256, dtype=F32),
            like(2, 256, 1024, dtype=F32),
            like(2, 1024, 256, dtype=F32),
            like(2, 256, 256, dtype=F32),
        ),
        in_specs=placed_anywhere(4) + whole(1),
        out_specs=whole(4),
        scratch_shapes=[pltpu.VMEM((4, 256, 1024), BF), pltpu.SemaphoreType.DMA((4,))],
        compiler_params=PARAMS,
        name="finish",
    )(f0, *far, tail)
    return (mixed, input_grad, grad_fu, grad_su, grad_fd, grad_sd)


def solution(mesh):
    placed = (
        P("dp", "chan"),
        P("chan", None, None),
        P("chan", None, None),
        P("chan", None, None),
        P("chan", None, None),
        P(),
        P(),
        P("dp", "chan"),
    )
    return jax.shard_map(
        per_device,
        mesh=mesh,
        in_specs=placed,
        out_specs=(
            P("dp", "chan"),
            P("dp", "chan"),
            P("chan", None, None),
            P("chan", None, None),
            P("chan", None, None),
            P("chan", None, None),
        ),
        check_vma=False,
    )
```

```python
import jax
import jax.numpy as jnp
from jax import lax
from jax.experimental import pallas as pl
from jax.experimental.pallas import tpu as pltpu
from jax.sharding import PartitionSpec as P

BF = jnp.bfloat16
F32 = jnp.float32
GELU_C = 0.7978845608028654
GELU_A = 0.044715


def nn(left, right):
    return lax.dot_general(left, right, (((1,), (0,)), ((), ())), preferred_element_type=F32)


def nt(left, right):
    return lax.dot_general(left, right, (((1,), (1,)), ((), ())), preferred_element_type=F32)


def tn(left, right):
    return lax.dot_general(left, right, (((0,), (0,)), ((), ())), preferred_element_type=F32)


def slot_order(perm_ref, me):
    rows, mine = [], []
    for i in range(4):
        rows.append(perm_ref[pl.ds(i, 16, stride=4), :])
        mine.append(perm_ref[pl.ds(4 * me + i, 1), :])
    perm = jnp.concatenate(rows, axis=1)
    own = jnp.concatenate(mine, axis=1)
    from_here = lax.shift_right_logical(perm, 9) == me
    from_group = lax.shift_right_logical(own, 9) == lax.broadcasted_iota(jnp.int32, (16, 512), 0)
    return from_here, (perm & 511).astype(F32), from_group


def ranks(hits):
    before = jnp.where(
        lax.broadcasted_iota(jnp.int32, (512, 512), 0) < lax.broadcasted_iota(jnp.int32, (512, 512), 1), 1.0, 0.0
    ).astype(BF)
    return jnp.where(hits, nn(jnp.where(hits, 1.0, 0.0).astype(BF), before), -1.0)


def source_matrix(perm_ref, me, ref):
    from_here, channel, _ = slot_order(perm_ref, me)
    rank = ranks(from_here)
    slot = lax.broadcasted_iota(jnp.int32, (32, 512), 0).astype(F32)
    lane = lax.broadcasted_iota(jnp.int32, (32, 512), 1).astype(F32)
    for r in range(16):
        hit = rank[r : r + 1, :] == slot
        source = jnp.sum(jnp.where(hit, channel[r : r + 1, :], 0.0), axis=1, keepdims=True)
        ref[32 * r : 32 * r + 32, :] = jnp.where(source == lane, 1.0, 0.0).astype(BF)


def target_matrix(perm_ref, me, ref):
    _, _, from_group = slot_order(perm_ref, me)
    rank = ranks(from_group)
    slot = lax.broadcasted_iota(jnp.int32, (32, 512), 0).astype(F32)
    for s in range(16):
        ref[32 * s : 32 * s + 32, :] = jnp.where(rank[s : s + 1, :] == slot, 1.0, 0.0).astype(BF)


def fold_up(source_ref, fu_ref, ref):
    for k in range(2):
        cols = slice(256 * k, 256 * k + 256)
        ref[:, cols] = nt(source_ref[:, cols], fu_ref[k]).astype(BF)


def fold_down(target_ref, sd_ref, ref):
    for k in range(2):
        cols = slice(256 * k, 256 * k + 256)
        ref[:, cols] = nn(target_ref[:, cols], sd_ref[k]).astype(BF)


def start(pairs, sems):
    copies = [pltpu.make_async_copy(source, target, sems.at[i]) for i, (source, target) in enumerate(pairs)]
    for copy in copies:
        copy.start()
    return copies


def send(source, target, sem):
    copy = pltpu.make_async_copy(source, target, sem)
    copy.start()
    return copy


def stage_one(
    tok_hbm, cot_hbm, fu_hbm, sd_hbm, pu_hbm, pd_hbm, out_hbm, tok, cot, fu, sd, pu, pd, matrix, weight, out, sems, out_sems
):
    pairs = ((pu_hbm, pu), (fu_hbm, fu), (tok_hbm, tok), (pd_hbm, pd), (sd_hbm, sd), (cot_hbm, cot))
    copies = start(pairs, sems)
    me = lax.axis_index("chan")
    copies[0].wait()
    source_matrix(pu, me, matrix.at[0])
    copies[1].wait()
    fold_up(matrix.at[0], fu, weight.at[0])
    copies[3].wait()
    target_matrix(pd, me, matrix.at[1])
    copies[4].wait()
    fold_down(matrix.at[1], sd, weight.at[1])
    sent = []
    for i, (wait, rows) in enumerate(((copies[2], tok), (copies[5], cot))):
        wait.wait()
        for j in range(2):
            groups = slice(8 * j, 8 * j + 8)
            part = nt(weight[i, 256 * j : 256 * j + 256, :], rows[...]).astype(BF)
            out[groups, 32 * i : 32 * i + 32, :] = part.reshape(8, 32, 1024)
            at = (groups, slice(32 * i, 32 * i + 32))
            sent.append(send(out.at[at], out_hbm.at[at], out_sems.at[2 * i + j]))
    for copy in sent:
        copy.wait()


def prepare(fu_ref, sd_ref, pu_ref, pd_ref, mark, up_src, up_tgt, down_src, down_tgt, w_up, w_down):
    me = lax.axis_index("chan")
    source_matrix(pu_ref, me, up_src)
    target_matrix(pu_ref, me, up_tgt)
    source_matrix(pd_ref, me, down_src)
    target_matrix(pd_ref, me, down_tgt)
    fold_up(up_src, fu_ref, w_up)
    fold_down(down_tgt, sd_ref, w_down)


def stage_two(
    tgt_hbm, src_hbm, su_hbm, fd_hbm, r_ref, out_hbm, f0, f1, f2, f3, s0, s1, s2, s3,
    up_tgt, down_src, su, fd, act, hg, nar, mix, pfd, psu, out, sems, out_sems,
):
    copies = start(((tgt_hbm, up_tgt), (src_hbm, down_src), (su_hbm, su), (fd_hbm, fd)), sems)
    copies[0].wait()
    mixed_in = tn(up_tgt[...], r_ref[:, 0:32, :].reshape(512, 1024)).astype(BF)
    copies[1].wait()
    nar_grad = tn(down_src[...], r_ref[:, 32:64, :].reshape(512, 1024)).astype(BF)
    copies[2].wait()
    copies[3].wait()
    z = lax.shift_right_logical(lax.axis_index("dp"), 1)
    sent = []
    for k in range(2):
        mi = mixed_in[256 * k : 256 * k + 256, :]
        ng = nar_grad[256 * k : 256 * k + 256, :]
        for c in range(2):
            units = slice(512 * c, 512 * c + 512)
            v = tn(su[k, :, units], mi)
            up = nn(fd[k, units, :], ng)
            sq = v * v
            h = 0.5 + 0.5 * jnp.tanh(v * (GELU_C + (GELU_C * GELU_A) * sq))
            a = (v * h).astype(BF)
            d = v * ((2 * GELU_C) + (6 * GELU_C * GELU_A) * sq)
            b = (up * (h * (1.0 + (1.0 - h) * d))).astype(BF)
            act[k, units, :] = a
            hg[k, units, :] = b
            gsu = nt(mi, b).astype(BF)
            gfd = nt(a, ng).astype(BF)
            for i in range(2):
                psu[2 * k + i, :, units] = gsu[128 * i : 128 * i + 128, :]
            for i in range(4):
                pfd[2 * k + c, :, 256 * i : 256 * i + 256] = gfd[128 * i : 128 * i + 128, :]
        if k == 1:
            for i, (f, s) in enumerate(((f0, s0), (f1, s1), (f2, s2), (f3, s3))):
                sent.append(send(pfd.at[(z + i) & 3], f, out_sems.at[i]))
                sent.append(send(psu.at[(z + i) & 3], s, out_sems.at[4 + i]))
        nar[256 * k : 256 * k + 256, :] = tn(fd[k], act[k]).astype(BF)
        mix[256 * k : 256 * k + 256, :] = nn(su[k], hg[k]).astype(BF)
    for i, (matrix, rows) in enumerate(((down_src, nar), (up_tgt, mix))):
        for j in range(2):
            groups = slice(8 * j, 8 * j + 8)
            part = nn(matrix[256 * j : 256 * j + 256, :], rows[...]).astype(BF)
            out[groups, 32 * i : 32 * i + 32, :] = part.reshape(8, 32, 1024)
            at = (groups, slice(32 * i, 32 * i + 32))
            sent.append(send(out.at[at], out_hbm.at[at], out_sems.at[8 + 2 * i + j]))
    for copy in sent:
        copy.wait()


def square_grads(
    tok_hbm, cot_hbm, src_hbm, tgt_hbm, r_ref, after, t_hbm, tok, cot, up_src, down_tgt, t, sems, out_sems
):
    top, low = slice(0, 512), slice(512, 1024)
    pairs = (
        (cot_hbm.at[top], cot.at[top]),
        (cot_hbm.at[low], cot.at[low]),
        (tgt_hbm, down_tgt),
        (tok_hbm.at[top], tok.at[top]),
        (tok_hbm.at[low], tok.at[low]),
        (src_hbm, up_src),
    )
    copies = start(pairs, sems)
    sent = []
    for n, rows in enumerate((cot, tok)):
        slots = r_ref[:, 32 * n : 32 * n + 32, :].reshape(512, 1024)
        copies[3 * n].wait()
        sums = nn(slots[:, top], rows[top, :])
        copies[3 * n + 1].wait()
        sums = (sums + nn(slots[:, low], rows[low, :])).astype(BF)
        copies[3 * n + 2].wait()
        for k in range(2):
            cols = slice(256 * k, 256 * k + 256)
            grad = tn(down_tgt[:, cols], sums[:, cols]) if n == 0 else tn(sums[:, cols], up_src[:, cols])
            grad = grad.astype(BF)
            for i in range(4):
                t[4 * k + i, :, 256 * n : 256 * n + 256] = grad[64 * i : 64 * i + 64, :]
        at = (slice(0, 8), slice(0, 64), slice(256 * n, 256 * n + 256))
        sent.append(send(t.at[at], t_hbm.at[at], out_sems.at[n]))
    for copy in sent:
        copy.wait()


def outputs(up_hbm, down_hbm, r_ref, after, mixed_ref, ig_ref, w_up, w_down, sems):
    copies = start(((down_hbm, w_down), (up_hbm, w_up)), sems)
    copies[0].wait()
    mixed_ref[...] = tn(r_ref[:, 0:32, :].reshape(512, 1024), w_down[...]).astype(BF)
    copies[1].wait()
    ig_ref[...] = tn(r_ref[:, 32:64, :].reshape(512, 1024), w_up[...]).astype(BF)


def total(t_ref, after, out_ref):
    sums = t_ref[0].astype(F32)
    for i in range(1, 8):
        sums = sums + t_ref[i].astype(F32)
    sums = sums.astype(BF)
    for i in range(8):
        out_ref[i] = sums


def finish_down(f0, f1, f2, f3, out_ref):
    z = lax.shift_right_logical(lax.axis_index("dp"), 1)
    for i, f in enumerate((f0, f1, f2, f3)):
        c = (z - i) & 3
        for b in range(4):
            out_ref[c >> 1, pl.ds((c & 1) * 512 + 128 * b, 128), :] = f[:, 256 * b : 256 * b + 256].astype(F32)


def finish_up(f0, f1, f2, f3, out_ref):
    z = lax.shift_right_logical(lax.axis_index("dp"), 1)
    for i, f in enumerate((f0, f1, f2, f3)):
        c = (z - i) & 3
        out_ref[c >> 1, pl.ds((c & 1) * 128, 128), :] = f[...].astype(F32)


def finish_square(t_ref, gfu_ref, gsd_ref):
    for k in range(2):
        for i in range(4):
            rows = slice(64 * i, 64 * i + 64)
            gsd_ref[k, rows, :] = t_ref[4 * k + i, :, 0:256].astype(F32)
            gfu_ref[k, rows, :] = t_ref[4 * k + i, :, 256:512].astype(F32)


def like(*shape, dtype=BF):
    return jax.ShapeDtypeStruct(shape, dtype)


def far(*shape):
    return pltpu.HBM(shape, BF)


def near(*shape):
    return pltpu.VMEM(shape, BF)


def placed(space, count):
    return [pl.BlockSpec(memory_space=space)] * count


def run(kernel, args, out_shape, mega, hbm=0, after=(), out_space=pltpu.VMEM, scratch=(), sems=(), flops=0, moved=0):
    args = tuple(pltpu.with_memory_space_constraint(x, pltpu.HBM) if i < hbm else x for i, x in enumerate(args))
    return pl.pallas_call(
        kernel,
        out_shape=out_shape,
        in_specs=placed(pltpu.HBM, hbm) + placed(pltpu.VMEM, len(args) - hbm) + placed(pl.ANY, len(after)),
        out_specs=placed(out_space, len(out_shape)),
        scratch_shapes=list(scratch) + [pltpu.SemaphoreType.DMA((n,)) for n in sems],
        compiler_params=pltpu.CompilerParams(vmem_limit_bytes=mega * 2**20),
        cost_estimate=pl.CostEstimate(flops=flops, bytes_accessed=moved, transcendentals=0),
        name=kernel.__name__,
    )(*args, *after)


def shift_z(step):
    return [(2 * z + x, 2 * ((z + step) % 4) + x) for z in range(4) for x in range(2)]


SWAP_X = [(2 * z + x, 2 * z + 1 - x) for z in range(4) for x in range(2)]


def exchange(values, axis):
    return lax.all_to_all(values, axis, split_axis=0, concat_axis=0, tiled=True)


def z_sum(parts):
    got = [lax.ppermute(part, "dp", shift_z(i)) for i, part in enumerate(parts) if i]
    sums = parts[0].astype(F32)
    for part in got:
        sums = sums + part.astype(F32)
    return sums.astype(BF)


def x_sum(part):
    return (part.astype(F32) + lax.ppermute(part, "dp", SWAP_X).astype(F32)).astype(BF)


def z_gather(part):
    return [part] + [lax.ppermute(part, "dp", shift_z(i)) for i in (1, 2, 3)]


def per_device(tokens, first_up, second_up, first_down, second_down, perm_up, perm_down, cotangent):
    perms = (perm_up.reshape(64, 128), perm_down.reshape(64, 128))
    square = near(512, 512)
    (sent,) = run(
        stage_one,
        (tokens, cotangent, first_up, second_down) + perms,
        (far(16, 64, 1024),),
        20,
        hbm=6,
        out_space=pltpu.HBM,
        scratch=[near(1024, 512)] * 2
        + [near(2, 256, 256)] * 2
        + [pltpu.VMEM((64, 128), jnp.int32)] * 2
        + [near(2, 512, 512)] * 2
        + [near(16, 64, 1024)],
        sems=(6, 4),
        flops=2 * 10**9,
        moved=5 * 10**6,
    )
    got = exchange(sent, "chan")
    up_src, up_tgt, down_src, down_tgt, w_up, w_down = run(
        prepare,
        (first_up, second_down) + perms,
        (far(512, 512),) * 6,
        20,
        after=(sent,),
        flops=2 * 10**9,
        moved=4 * 10**6,
    )
    sent, *grads = run(
        stage_two,
        (up_tgt, down_src, second_up, first_down, got),
        (far(16, 64, 1024),) + (far(128, 1024),) * 8,
        32,
        hbm=4,
        out_space=pltpu.HBM,
        scratch=[square, square, near(2, 256, 1024), near(2, 1024, 256)]
        + [near(2, 1024, 1024)] * 2
        + [near(512, 1024)] * 2
        + [near(4, 128, 1024)] * 2
        + [near(16, 64, 1024)],
        sems=(4, 12),
        flops=85 * 10**8,
        moved=9 * 10**6,
    )
    got = exchange(sent, "chan")
    down_part = z_sum(grads[:4])
    up_part = z_sum(grads[4:])
    (tail,) = run(
        square_grads,
        (tokens, cotangent, up_src, down_tgt, got),
        (far(8, 64, 512),),
        20,
        hbm=4,
        after=(up_part,),
        out_space=pltpu.HBM,
        scratch=[near(1024, 512)] * 2 + [square, square, near(8, 64, 512)],
        sems=(6, 2),
        flops=16 * 10**8,
        moved=5 * 10**6,
    )
    down_all = z_gather(x_sum(down_part))
    up_all = z_gather(x_sum(up_part))
    tail_parts = exchange(tail, "dp")
    mixed, input_grad = run(
        outputs,
        (w_up, w_down, got),
        (like(1024, 512),) * 2,
        20,
        hbm=2,
        after=(tail,),
        scratch=[square, square],
        sems=(2,),
        flops=10**9,
        moved=5 * 10**6,
    )
    (tail_sums,) = run(
        total, (tail_parts,), (far(8, 64, 512),), 20, after=(mixed,), flops=10**6, moved=10**6
    )
    tail_all = exchange(tail_sums, "dp")
    (grad_fd,) = run(finish_down, down_all, (like(2, 1024, 256, dtype=F32),), 20, flops=10**6, moved=3 * 10**6)
    (grad_su,) = run(finish_up, up_all, (like(2, 256, 1024, dtype=F32),), 20, flops=10**6, moved=3 * 10**6)
    grad_fu, grad_sd = run(
        finish_square, (tail_all,), (like(2, 256, 256, dtype=F32),) * 2, 20, flops=10**6, moved=2 * 10**6
    )
    return (mixed, input_grad, grad_fu, grad_su, grad_fd, grad_sd)


def solution(mesh):
    layout = (
        P("dp", "chan"),
        P("chan", None, None),
        P("chan", None, None),
        P("chan", None, None),
        P("chan", None, None),
        P(),
        P(),
        P("dp", "chan"),
    )
    return jax.shard_map(
        per_device,
        mesh=mesh,
        in_specs=layout,
        out_specs=(
            P("dp", "chan"),
            P("dp", "chan"),
            P("chan", None, None),
            P("chan", None, None),
            P("chan", None, None),
            P("chan", None, None),
        ),
        check_vma=False,
    )
```

```python
import jax
import jax.numpy as jnp
from jax import lax
from jax.experimental import pallas as pl
from jax.experimental.pallas import tpu as pltpu
from jax.sharding import PartitionSpec as P

BF = jnp.bfloat16
F32 = jnp.float32
GELU_C = 0.7978845608028654
GELU_A = 0.044715


def nn(left, right):
    return lax.dot_general(left, right, (((1,), (0,)), ((), ())), preferred_element_type=F32)


def nt(left, right):
    return lax.dot_general(left, right, (((1,), (1,)), ((), ())), preferred_element_type=F32)


def tn(left, right):
    return lax.dot_general(left, right, (((0,), (0,)), ((), ())), preferred_element_type=F32)


def slot_order(perm_ref, me):
    rows, mine = [], []
    for i in range(4):
        rows.append(perm_ref[pl.ds(i, 16, stride=4), :])
        mine.append(perm_ref[pl.ds(4 * me + i, 1), :])
    perm = jnp.concatenate(rows, axis=1)
    own = jnp.concatenate(mine, axis=1)
    from_here = lax.shift_right_logical(perm, 9) == me
    from_group = lax.shift_right_logical(own, 9) == lax.broadcasted_iota(jnp.int32, (16, 512), 0)
    return from_here, (perm & 511).astype(F32), from_group


def ranks(hits):
    before = jnp.where(
        lax.broadcasted_iota(jnp.int32, (512, 512), 0) < lax.broadcasted_iota(jnp.int32, (512, 512), 1), 1.0, 0.0
    ).astype(BF)
    return jnp.where(hits, nn(jnp.where(hits, 1.0, 0.0).astype(BF), before), -1.0)


def source_matrix(perm_ref, me, ref):
    from_here, channel, _ = slot_order(perm_ref, me)
    rank = ranks(from_here)
    slot = lax.broadcasted_iota(jnp.int32, (32, 512), 0).astype(F32)
    lane = lax.broadcasted_iota(jnp.int32, (32, 512), 1).astype(F32)
    for r in range(16):
        hit = rank[r : r + 1, :] == slot
        source = jnp.sum(jnp.where(hit, channel[r : r + 1, :], 0.0), axis=1, keepdims=True)
        ref[32 * r : 32 * r + 32, :] = jnp.where(source == lane, 1.0, 0.0).astype(BF)


def target_matrix(perm_ref, me, ref):
    _, _, from_group = slot_order(perm_ref, me)
    rank = ranks(from_group)
    slot = lax.broadcasted_iota(jnp.int32, (32, 512), 0).astype(F32)
    for s in range(16):
        ref[32 * s : 32 * s + 32, :] = jnp.where(rank[s : s + 1, :] == slot, 1.0, 0.0).astype(BF)


def fold_up(source_ref, fu_ref, ref):
    for k in range(2):
        cols = slice(256 * k, 256 * k + 256)
        ref[:, cols] = nt(source_ref[:, cols], fu_ref[k]).astype(BF)


def fold_down(target_ref, sd_ref, ref):
    for k in range(2):
        cols = slice(256 * k, 256 * k + 256)
        ref[:, cols] = nn(target_ref[:, cols], sd_ref[k]).astype(BF)


def start(pairs, sems):
    copies = [pltpu.make_async_copy(source, target, sems.at[i]) for i, (source, target) in enumerate(pairs)]
    for copy in copies:
        copy.start()
    return copies


def send(source, target, sem):
    copy = pltpu.make_async_copy(source, target, sem)
    copy.start()
    return copy


def stage_one(
    tok_hbm, cot_hbm, fu_hbm, sd_hbm, pu_hbm, pd_hbm, out_hbm, tok, cot, fu, sd, pu, pd, matrix, weight, out, sems, out_sems
):
    pairs = ((pu_hbm, pu), (fu_hbm, fu), (tok_hbm, tok), (pd_hbm, pd), (sd_hbm, sd), (cot_hbm, cot))
    copies = start(pairs, sems)
    me = lax.axis_index("chan")
    copies[0].wait()
    source_matrix(pu, me, matrix.at[0])
    copies[1].wait()
    fold_up(matrix.at[0], fu, weight.at[0])
    copies[3].wait()
    target_matrix(pd, me, matrix.at[1])
    copies[4].wait()
    fold_down(matrix.at[1], sd, weight.at[1])
    sent = []
    for i, (wait, rows) in enumerate(((copies[2], tok), (copies[5], cot))):
        wait.wait()
        for j in range(2):
            groups = slice(8 * j, 8 * j + 8)
            part = nt(weight[i, 256 * j : 256 * j + 256, :], rows[...]).astype(BF)
            out[groups, 32 * i : 32 * i + 32, :] = part.reshape(8, 32, 1024)
            at = (groups, slice(32 * i, 32 * i + 32))
            sent.append(send(out.at[at], out_hbm.at[at], out_sems.at[2 * i + j]))
    for copy in sent:
        copy.wait()


def prepare(fu_ref, sd_ref, pu_ref, pd_ref, mark, up_src, up_tgt, down_src, down_tgt, w_up, w_down):
    me = lax.axis_index("chan")
    source_matrix(pu_ref, me, up_src)
    target_matrix(pu_ref, me, up_tgt)
    source_matrix(pd_ref, me, down_src)
    target_matrix(pd_ref, me, down_tgt)
    fold_up(up_src, fu_ref, w_up)
    fold_down(down_tgt, sd_ref, w_down)


def stage_two(
    tgt_hbm, src_hbm, su_hbm, fd_hbm, r_ref, out_hbm, f0, f1, f2, f3, s0, s1, s2, s3,
    up_tgt, down_src, su, fd, act, hg, nar, mix, pfd, psu, out, sems, out_sems,
):
    copies = start(((tgt_hbm, up_tgt), (src_hbm, down_src)), sems)
    copies[0].wait()
    copies += [send(su_hbm, su, sems.at[2]), send(fd_hbm, fd, sems.at[3])]
    mixed_in = tn(up_tgt[...], r_ref[:, 0:32, :].reshape(512, 1024)).astype(BF)
    copies[1].wait()
    nar_grad = tn(down_src[...], r_ref[:, 32:64, :].reshape(512, 1024)).astype(BF)
    copies[2].wait()
    copies[3].wait()
    z = lax.shift_right_logical(lax.axis_index("dp"), 1)
    sent = []
    for k in range(2):
        mi = mixed_in[256 * k : 256 * k + 256, :]
        ng = nar_grad[256 * k : 256 * k + 256, :]
        for c in range(2):
            units = slice(512 * c, 512 * c + 512)
            v = tn(su[k, :, units], mi)
            up = nn(fd[k, units, :], ng)
            sq = v * v
            h = 0.5 + 0.5 * jnp.tanh(v * (GELU_C + (GELU_C * GELU_A) * sq))
            a = (v * h).astype(BF)
            d = v * ((2 * GELU_C) + (6 * GELU_C * GELU_A) * sq)
            b = (up * (h * (1.0 + (1.0 - h) * d))).astype(BF)
            act[k, units, :] = a
            hg[k, units, :] = b
            gsu = nt(mi, b).astype(BF)
            gfd = nt(a, ng).astype(BF)
            for i in range(2):
                psu[2 * k + i, :, units] = gsu[128 * i : 128 * i + 128, :]
            for i in range(4):
                pfd[2 * k + c, :, 256 * i : 256 * i + 256] = gfd[128 * i : 128 * i + 128, :]
        if k == 1:
            for i, (f, s) in enumerate(((f0, s0), (f1, s1), (f2, s2), (f3, s3))):
                sent.append(send(pfd.at[(z + i) & 3], f, out_sems.at[i]))
                sent.append(send(psu.at[(z + i) & 3], s, out_sems.at[4 + i]))
        nar[256 * k : 256 * k + 256, :] = tn(fd[k], act[k]).astype(BF)
        mix[256 * k : 256 * k + 256, :] = nn(su[k], hg[k]).astype(BF)
    for i, (matrix, rows) in enumerate(((down_src, nar), (up_tgt, mix))):
        for j in range(2):
            groups = slice(8 * j, 8 * j + 8)
            part = nn(matrix[256 * j : 256 * j + 256, :], rows[...]).astype(BF)
            out[groups, 32 * i : 32 * i + 32, :] = part.reshape(8, 32, 1024)
            at = (groups, slice(32 * i, 32 * i + 32))
            sent.append(send(out.at[at], out_hbm.at[at], out_sems.at[8 + 2 * i + j]))
    for copy in sent:
        copy.wait()


def square_grads(
    tok_hbm, cot_hbm, src_hbm, tgt_hbm, r_ref, t_hbm, tok, cot, up_src, down_tgt, t, sems, out_sems
):
    top, low = slice(0, 512), slice(512, 1024)
    pairs = (
        (cot_hbm.at[top], cot.at[top]),
        (cot_hbm.at[low], cot.at[low]),
        (tgt_hbm, down_tgt),
        (tok_hbm.at[top], tok.at[top]),
        (tok_hbm.at[low], tok.at[low]),
        (src_hbm, up_src),
    )
    copies = start(pairs, sems)
    sent = []
    for n, rows in enumerate((cot, tok)):
        slots = r_ref[:, 32 * n : 32 * n + 32, :].reshape(512, 1024)
        copies[3 * n].wait()
        sums = nn(slots[:, top], rows[top, :])
        copies[3 * n + 1].wait()
        sums = (sums + nn(slots[:, low], rows[low, :])).astype(BF)
        copies[3 * n + 2].wait()
        for k in range(2):
            cols = slice(256 * k, 256 * k + 256)
            grad = tn(down_tgt[:, cols], sums[:, cols]) if n == 0 else tn(sums[:, cols], up_src[:, cols])
            grad = grad.astype(BF)
            for i in range(4):
                t[4 * k + i, :, 256 * n : 256 * n + 256] = grad[64 * i : 64 * i + 64, :]
        at = (slice(0, 8), slice(0, 64), slice(256 * n, 256 * n + 256))
        sent.append(send(t.at[at], t_hbm.at[at], out_sems.at[n]))
    for copy in sent:
        copy.wait()


def outputs(up_hbm, down_hbm, r_ref, after, mixed_ref, ig_ref, w_up, w_down, sems):
    copies = start(((down_hbm, w_down), (up_hbm, w_up)), sems)
    copies[0].wait()
    mixed_ref[...] = tn(r_ref[:, 0:32, :].reshape(512, 1024), w_down[...]).astype(BF)
    copies[1].wait()
    ig_ref[...] = tn(r_ref[:, 32:64, :].reshape(512, 1024), w_up[...]).astype(BF)


def total(t_ref, after, out_ref):
    sums = t_ref[0].astype(F32)
    for i in range(1, 8):
        sums = sums + t_ref[i].astype(F32)
    sums = sums.astype(BF)
    for i in range(8):
        out_ref[i] = sums


def place(part_f, part_s, step, fd, su, fd_hbm, su_hbm, sems):
    for b in range(4):
        fd[128 * b : 128 * b + 128, :] = part_f[:, 256 * b : 256 * b + 256].astype(F32)
    su[...] = part_s[...].astype(F32)
    c = (lax.shift_right_logical(lax.axis_index("dp"), 1) - step) & 3
    fd_at = fd_hbm.at[c >> 1, pl.ds(pl.multiple_of((c & 1) * 512, 512), 512)]
    su_at = su_hbm.at[c >> 1, pl.ds(pl.multiple_of((c & 1) * 128, 128), 128)]
    return start(((fd, fd_at), (su, su_at)), sems)


def place_near(own, left, right, fd_hbm, su_hbm, fd, su, sems):
    sent = []
    for n, (part, step) in enumerate(((own, 0), (left, 1), (right, 3))):
        halves = (part.at[0:128], part.at[128:256])
        sent += place(*halves, step, fd.at[n], su.at[n], fd_hbm, su_hbm, sems.at[n])
    for copy in sent:
        copy.wait()


def finish(f_far, s_far, t_ref, fd_in, su_in, fd_hbm, su_hbm, gfu_hbm, gsd_hbm, fd, su, gfu, gsd, sems, more_sems):
    sent = place(f_far, s_far, 2, fd, su, fd_hbm, su_hbm, sems)
    for k in range(2):
        for i in range(4):
            rows = slice(64 * i, 64 * i + 64)
            gsd[k, rows, :] = t_ref[4 * k + i, :, 0:256].astype(F32)
            gfu[k, rows, :] = t_ref[4 * k + i, :, 256:512].astype(F32)
    sent += start(((gfu, gfu_hbm), (gsd, gsd_hbm)), more_sems)
    for copy in sent:
        copy.wait()


def like(*shape, dtype=BF):
    return jax.ShapeDtypeStruct(shape, dtype)


def far(*shape):
    return pltpu.HBM(shape, BF)


def near(*shape):
    return pltpu.VMEM(shape, BF)


def placed(space, count):
    return [pl.BlockSpec(memory_space=space)] * count


def run(kernel, args, out_shape, mega, hbm=0, after=(), out_space=pltpu.VMEM, aliases=None, scratch=(), sems=(), flops=0, moved=0):
    args = tuple(pltpu.with_memory_space_constraint(x, pltpu.HBM) if i < hbm else x for i, x in enumerate(args))
    if not aliases:
        after = tuple(pltpu.with_memory_space_constraint(x, pltpu.HBM) for x in after)
    return pl.pallas_call(
        kernel,
        out_shape=out_shape,
        in_specs=placed(pltpu.HBM, hbm) + placed(pltpu.VMEM, len(args) - hbm) + placed(pl.ANY if aliases else pltpu.HBM, len(after)),
        out_specs=placed(out_space, len(out_shape)),
        input_output_aliases=aliases or {},
        scratch_shapes=list(scratch) + [pltpu.SemaphoreType.DMA(n if isinstance(n, tuple) else (n,)) for n in sems],
        compiler_params=pltpu.CompilerParams(vmem_limit_bytes=mega * 2**20),
        cost_estimate=pl.CostEstimate(flops=flops, bytes_accessed=moved, transcendentals=0),
        name=kernel.__name__,
    )(*args, *after)


def shift_z(step):
    return [(2 * z + x, 2 * ((z + step) % 4) + x) for z in range(4) for x in range(2)]


SWAP_X = [(2 * z + x, 2 * z + 1 - x) for z in range(4) for x in range(2)]


def exchange(values, axis):
    return lax.all_to_all(values, axis, split_axis=0, concat_axis=0, tiled=True)


def shifted(part, step):
    return lax.ppermute(part, "dp", shift_z(step))


def added(*parts):
    sums = parts[0].astype(F32)
    for part in parts[1:]:
        sums = sums + part.astype(F32)
    return sums.astype(BF)


def z_sums(f, s):
    f_on = shifted(f[2], 1)
    s_on = shifted(s[2], 3)
    s_got = shifted(s[1], 1)
    f_got = shifted(f[3], 3)
    f_far = shifted(added(f[1], f_on), 1)
    s_far = shifted(added(s[3], s_on), 3)
    return added(f[0], f_got, f_far), added(s[0], s_got, s_far)


def per_device(tokens, first_up, second_up, first_down, second_down, perm_up, perm_down, cotangent):
    perms = (perm_up.reshape(64, 128), perm_down.reshape(64, 128))
    square = near(512, 512)
    (sent,) = run(
        stage_one,
        (tokens, cotangent, first_up, second_down) + perms,
        (far(16, 64, 1024),),
        20,
        hbm=6,
        out_space=pltpu.HBM,
        scratch=[near(1024, 512)] * 2
        + [near(2, 256, 256)] * 2
        + [pltpu.VMEM((64, 128), jnp.int32)] * 2
        + [near(2, 512, 512)] * 2
        + [near(16, 64, 1024)],
        sems=(6, 4),
        flops=2 * 10**9,
        moved=5 * 10**6,
    )
    got = exchange(sent, "chan")
    up_src, up_tgt, down_src, down_tgt, w_up, w_down = run(
        prepare,
        (first_up, second_down) + perms,
        (far(512, 512),) * 6,
        20,
        after=(sent,),
        flops=2 * 10**9,
        moved=4 * 10**6,
    )
    sent, *grads = run(
        stage_two,
        (up_tgt, down_src, second_up, first_down, got),
        (far(16, 64, 1024),) + (far(128, 1024),) * 8,
        32,
        hbm=4,
        out_space=pltpu.HBM,
        scratch=[square, square, near(2, 256, 1024), near(2, 1024, 256)]
        + [near(2, 1024, 1024)] * 2
        + [near(512, 1024)] * 2
        + [near(4, 128, 1024)] * 2
        + [near(16, 64, 1024)],
        sems=(4, 12),
        flops=85 * 10**8,
        moved=9 * 10**6,
    )
    got = exchange(sent, "chan")
    part = jnp.concatenate(z_sums(grads[:4], grads[4:]))
    chunk = added(part, lax.ppermute(part, "dp", SWAP_X))
    left, right = shifted(chunk, 1), shifted(chunk, 3)
    f_far, s_far = shifted(left[:128], 1), shifted(right[128:], 3)
    (tail,) = run(
        square_grads,
        (tokens, cotangent, up_src, down_tgt, got),
        (far(8, 64, 512),),
        20,
        hbm=4,
        out_space=pltpu.HBM,
        scratch=[near(1024, 512)] * 2 + [square, square, near(8, 64, 512)],
        sems=(6, 2),
        flops=16 * 10**8,
        moved=5 * 10**6,
    )
    tail_parts = exchange(tail, "dp")
    mixed, input_grad = run(
        outputs,
        (w_up, w_down, got),
        (like(1024, 512),) * 2,
        20,
        hbm=2,
        after=(tail,),
        scratch=[square, square],
        sems=(2,),
        flops=10**9,
        moved=5 * 10**6,
    )
    (tail_sums,) = run(
        total, (tail_parts,), (far(8, 64, 512),), 20, after=(mixed,), flops=10**6, moved=10**6
    )
    tail_all = exchange(tail_sums, "dp")
    wide = (like(2, 1024, 256, dtype=F32), like(2, 256, 1024, dtype=F32))
    held = run(
        place_near,
        (chunk, left, right),
        wide,
        24,
        out_space=pl.ANY,
        scratch=[pltpu.VMEM((3, 512, 256), F32), pltpu.VMEM((3, 128, 1024), F32)],
        sems=((3, 2),),
        flops=10**6,
        moved=5 * 10**6,
    )
    small = like(2, 256, 256, dtype=F32)
    grad_fd, grad_su, grad_fu, grad_sd = run(
        finish,
        (f_far, s_far, tail_all),
        wide + (small, small),
        24,
        after=tuple(held),
        out_space=pl.ANY,
        aliases={3: 0, 4: 1},
        scratch=[pltpu.VMEM((512, 256), F32), pltpu.VMEM((128, 1024), F32)] + [pltpu.VMEM((2, 256, 256), F32)] * 2,
        sems=((2,), (2,)),
        flops=10**6,
        moved=4 * 10**6,
    )
    return (mixed, input_grad, grad_fu, grad_su, grad_fd, grad_sd)


def solution(mesh):
    layout = (
        P("dp", "chan"),
        P("chan", None, None),
        P("chan", None, None),
        P("chan", None, None),
        P("chan", None, None),
        P(),
        P(),
        P("dp", "chan"),
    )
    return jax.shard_map(
        per_device,
        mesh=mesh,
        in_specs=layout,
        out_specs=(
            P("dp", "chan"),
            P("dp", "chan"),
            P("chan", None, None),
            P("chan", None, None),
            P("chan", None, None),
            P("chan", None, None),
        ),
        check_vma=False,
    )
```

```python
import jax
import jax.numpy as jnp
from jax import lax
from jax.experimental import pallas as pl
from jax.experimental.pallas import tpu as pltpu
from jax.sharding import PartitionSpec as P

BF = jnp.bfloat16
F32 = jnp.float32
GELU_C = 0.7978845608028654
GELU_A = 0.044715


def nn(left, right):
    return lax.dot_general(left, right, (((1,), (0,)), ((), ())), preferred_element_type=F32)


def nt(left, right):
    return lax.dot_general(left, right, (((1,), (1,)), ((), ())), preferred_element_type=F32)


def tn(left, right):
    return lax.dot_general(left, right, (((0,), (0,)), ((), ())), preferred_element_type=F32)


def slot_order(perm_ref, me):
    rows, mine = [], []
    for i in range(4):
        rows.append(perm_ref[pl.ds(i, 16, stride=4), :])
        mine.append(perm_ref[pl.ds(4 * me + i, 1), :])
    perm = jnp.concatenate(rows, axis=1)
    own = jnp.concatenate(mine, axis=1)
    from_here = lax.shift_right_logical(perm, 9) == me
    from_group = lax.shift_right_logical(own, 9) == lax.broadcasted_iota(jnp.int32, (16, 512), 0)
    return from_here, (perm & 511).astype(F32), from_group


def ranks(hits):
    before = jnp.where(
        lax.broadcasted_iota(jnp.int32, (512, 512), 0) < lax.broadcasted_iota(jnp.int32, (512, 512), 1), 1.0, 0.0
    ).astype(BF)
    return jnp.where(hits, nn(jnp.where(hits, 1.0, 0.0).astype(BF), before), -1.0)


def source_matrix(perm_ref, me, ref):
    from_here, channel, _ = slot_order(perm_ref, me)
    rank = ranks(from_here)
    slot = lax.broadcasted_iota(jnp.int32, (32, 512), 0).astype(F32)
    lane = lax.broadcasted_iota(jnp.int32, (32, 512), 1).astype(F32)
    for r in range(16):
        hit = rank[r : r + 1, :] == slot
        source = jnp.sum(jnp.where(hit, channel[r : r + 1, :], 0.0), axis=1, keepdims=True)
        ref[32 * r : 32 * r + 32, :] = jnp.where(source == lane, 1.0, 0.0).astype(BF)


def target_matrix(perm_ref, me, ref):
    _, _, from_group = slot_order(perm_ref, me)
    rank = ranks(from_group)
    slot = lax.broadcasted_iota(jnp.int32, (32, 512), 0).astype(F32)
    for s in range(16):
        ref[32 * s : 32 * s + 32, :] = jnp.where(rank[s : s + 1, :] == slot, 1.0, 0.0).astype(BF)


def fold_up(source_ref, fu_ref, ref):
    for k in range(2):
        cols = slice(256 * k, 256 * k + 256)
        ref[:, cols] = nt(source_ref[:, cols], fu_ref[k]).astype(BF)


def fold_down(target_ref, sd_ref, ref):
    for k in range(2):
        cols = slice(256 * k, 256 * k + 256)
        ref[:, cols] = nn(target_ref[:, cols], sd_ref[k]).astype(BF)


def start(pairs, sems):
    copies = [pltpu.make_async_copy(source, target, sems.at[i]) for i, (source, target) in enumerate(pairs)]
    for copy in copies:
        copy.start()
    return copies


def send(source, target, sem):
    copy = pltpu.make_async_copy(source, target, sem)
    copy.start()
    return copy


def stage_one(
    tok_hbm, cot_hbm, fu_hbm, sd_hbm, pu_hbm, pd_hbm, out_hbm, tok, cot, fu, sd, pu, pd, matrix, weight, out, sems, out_sems
):
    pairs = ((pu_hbm, pu), (fu_hbm, fu), (tok_hbm, tok), (pd_hbm, pd), (sd_hbm, sd), (cot_hbm, cot))
    copies = start(pairs, sems)
    me = lax.axis_index("chan")
    copies[0].wait()
    source_matrix(pu, me, matrix.at[0])
    copies[1].wait()
    fold_up(matrix.at[0], fu, weight.at[0])
    copies[3].wait()
    target_matrix(pd, me, matrix.at[1])
    copies[4].wait()
    fold_down(matrix.at[1], sd, weight.at[1])
    sent = []
    for i, (wait, rows) in enumerate(((copies[2], tok), (copies[5], cot))):
        wait.wait()
        for j in range(2):
            groups = slice(8 * j, 8 * j + 8)
            part = nt(weight[i, 256 * j : 256 * j + 256, :], rows[...]).astype(BF)
            out[groups, 32 * i : 32 * i + 32, :] = part.reshape(8, 32, 1024)
            at = (groups, slice(32 * i, 32 * i + 32))
            sent.append(send(out.at[at], out_hbm.at[at], out_sems.at[2 * i + j]))
    for copy in sent:
        copy.wait()


def prepare(fu_ref, sd_ref, pu_ref, pd_ref, mark, up_src, up_tgt, down_src, down_tgt, w_up, w_down):
    me = lax.axis_index("chan")
    source_matrix(pu_ref, me, up_src)
    target_matrix(pu_ref, me, up_tgt)
    source_matrix(pd_ref, me, down_src)
    target_matrix(pd_ref, me, down_tgt)
    fold_up(up_src, fu_ref, w_up)
    fold_down(down_tgt, sd_ref, w_down)


def stage_two(
    src_hbm, su_hbm, fd_hbm, up_tgt, r_ref, out_hbm, f0, f1, f2, f3, s0, s1, s2, s3,
    down_src, su, fd, act, hg, nar, mix, pfd, psu, out, sems, out_sems,
):
    copies = start(((src_hbm, down_src), (su_hbm, su), (fd_hbm, fd)), sems)
    mixed_in = tn(up_tgt[...], r_ref[:, 0:32, :].reshape(512, 1024)).astype(BF)
    copies[0].wait()
    nar_grad = tn(down_src[...], r_ref[:, 32:64, :].reshape(512, 1024)).astype(BF)
    copies[1].wait()
    copies[2].wait()
    z = lax.shift_right_logical(lax.axis_index("dp"), 1)
    sent = []
    for k in range(2):
        mi = mixed_in[256 * k : 256 * k + 256, :]
        ng = nar_grad[256 * k : 256 * k + 256, :]
        for c in range(2):
            units = slice(512 * c, 512 * c + 512)
            v = tn(su[k, :, units], mi)
            up = nn(fd[k, units, :], ng)
            sq = v * v
            h = 0.5 + 0.5 * jnp.tanh(v * (GELU_C + (GELU_C * GELU_A) * sq))
            a = (v * h).astype(BF)
            d = v * ((2 * GELU_C) + (6 * GELU_C * GELU_A) * sq)
            b = (up * (h * (1.0 + (1.0 - h) * d))).astype(BF)
            act[k, units, :] = a
            hg[k, units, :] = b
            gsu = nt(mi, b).astype(BF)
            gfd = nt(a, ng).astype(BF)
            for i in range(2):
                psu[2 * k + i, :, units] = gsu[128 * i : 128 * i + 128, :]
            for i in range(4):
                pfd[2 * k + c, :, 256 * i : 256 * i + 256] = gfd[128 * i : 128 * i + 128, :]
        if k == 1:
            for i, (f, s) in enumerate(((f0, s0), (f1, s1), (f2, s2), (f3, s3))):
                sent.append(send(pfd.at[(z + i) & 3], f, out_sems.at[i]))
                sent.append(send(psu.at[(z + i) & 3], s, out_sems.at[4 + i]))
        nar[256 * k : 256 * k + 256, :] = tn(fd[k], act[k]).astype(BF)
        mix[256 * k : 256 * k + 256, :] = nn(su[k], hg[k]).astype(BF)
    for i, (matrix, rows) in enumerate(((down_src, nar), (up_tgt, mix))):
        for j in range(4):
            groups = slice(4 * j, 4 * j + 4)
            part = nn(matrix[128 * j : 128 * j + 128, :], rows[...]).astype(BF)
            out[groups, 32 * i : 32 * i + 32, :] = part.reshape(4, 32, 1024)
            at = (groups, slice(32 * i, 32 * i + 32))
            sent.append(send(out.at[at], out_hbm.at[at], out_sems.at[8 + 4 * i + j]))
    for copy in sent:
        copy.wait()


def square_grads(
    tok_hbm, cot_hbm, src_hbm, tgt_hbm, r_ref, t_hbm, tok, cot, up_src, down_tgt, t, sems, out_sems
):
    top, low = slice(0, 512), slice(512, 1024)
    pairs = (
        (cot_hbm.at[top], cot.at[top]),
        (cot_hbm.at[low], cot.at[low]),
        (tgt_hbm, down_tgt),
        (tok_hbm.at[top], tok.at[top]),
        (tok_hbm.at[low], tok.at[low]),
        (src_hbm, up_src),
    )
    copies = start(pairs, sems)
    sent = []
    for n, rows in enumerate((cot, tok)):
        slots = r_ref[:, 32 * n : 32 * n + 32, :].reshape(512, 1024)
        copies[3 * n].wait()
        sums = nn(slots[:, top], rows[top, :])
        copies[3 * n + 1].wait()
        sums = (sums + nn(slots[:, low], rows[low, :])).astype(BF)
        copies[3 * n + 2].wait()
        for k in range(2):
            cols = slice(256 * k, 256 * k + 256)
            grad = tn(down_tgt[:, cols], sums[:, cols]) if n == 0 else tn(sums[:, cols], up_src[:, cols])
            grad = grad.astype(BF)
            for i in range(4):
                t[4 * k + i, :, 256 * n : 256 * n + 256] = grad[64 * i : 64 * i + 64, :]
        at = (slice(0, 8), slice(0, 64), slice(256 * n, 256 * n + 256))
        sent.append(send(t.at[at], t_hbm.at[at], out_sems.at[n]))
    for copy in sent:
        copy.wait()


def outputs(up_hbm, down_hbm, r_ref, after, mixed_ref, ig_ref, w_up, w_down, sems):
    copies = start(((down_hbm, w_down), (up_hbm, w_up)), sems)
    copies[0].wait()
    mixed_ref[...] = tn(r_ref[:, 0:32, :].reshape(512, 1024), w_down[...]).astype(BF)
    copies[1].wait()
    ig_ref[...] = tn(r_ref[:, 32:64, :].reshape(512, 1024), w_up[...]).astype(BF)


def total(t_ref, after, out_ref):
    sums = t_ref[0].astype(F32)
    for i in range(1, 8):
        sums = sums + t_ref[i].astype(F32)
    sums = sums.astype(BF)
    for i in range(8):
        out_ref[i] = sums


def join(f0, f1, f2, s0, s1, s2, out_ref):
    out_ref[0:128, :] = (f0[...].astype(F32) + f1[...].astype(F32) + f2[...].astype(F32)).astype(BF)
    out_ref[128:256, :] = (s0[...].astype(F32) + s1[...].astype(F32) + s2[...].astype(F32)).astype(BF)


def pair(mine, other, out_ref):
    out_ref[...] = (mine[...].astype(F32) + other[...].astype(F32)).astype(BF)


def halves(left, right, f_out, s_out):
    f_out[...] = left[0:128, :]
    s_out[...] = right[128:256, :]


def place(part_f, part_s, step, fd, su, fd_hbm, su_hbm, sems):
    for b in range(4):
        fd[128 * b : 128 * b + 128, :] = part_f[:, 256 * b : 256 * b + 256].astype(F32)
    su[...] = part_s[...].astype(F32)
    c = (lax.shift_right_logical(lax.axis_index("dp"), 1) - step) & 3
    fd_at = fd_hbm.at[c >> 1, pl.ds(pl.multiple_of((c & 1) * 512, 512), 512)]
    su_at = su_hbm.at[c >> 1, pl.ds(pl.multiple_of((c & 1) * 128, 128), 128)]
    return start(((fd, fd_at), (su, su_at)), sems)


def place_near(own, left, right, fd_hbm, su_hbm, fd, su, sems):
    sent = []
    for n, (part, step) in enumerate(((own, 0), (left, 1), (right, 3))):
        halves = (part.at[0:128], part.at[128:256])
        sent += place(*halves, step, fd.at[n], su.at[n], fd_hbm, su_hbm, sems.at[n])
    for copy in sent:
        copy.wait()


def finish(f_far, s_far, t_ref, fd_in, su_in, fd_hbm, su_hbm, gfu_hbm, gsd_hbm, fd, su, gfu, gsd, sems, more_sems):
    sent = place(f_far, s_far, 2, fd, su, fd_hbm, su_hbm, sems)
    for k in range(2):
        for i in range(4):
            rows = slice(64 * i, 64 * i + 64)
            gsd[k, rows, :] = t_ref[4 * k + i, :, 0:256].astype(F32)
            gfu[k, rows, :] = t_ref[4 * k + i, :, 256:512].astype(F32)
    sent += start(((gfu, gfu_hbm), (gsd, gsd_hbm)), more_sems)
    for copy in sent:
        copy.wait()


def like(*shape, dtype=BF):
    return jax.ShapeDtypeStruct(shape, dtype)


def far(*shape):
    return pltpu.HBM(shape, BF)


def near(*shape):
    return pltpu.VMEM(shape, BF)


def placed(space, count):
    return [pl.BlockSpec(memory_space=space)] * count


def run(kernel, args, out_shape, mega, hbm=0, after=(), out_space=pltpu.VMEM, aliases=None, scratch=(), sems=(), flops=0, moved=0):
    args = tuple(pltpu.with_memory_space_constraint(x, pltpu.HBM) if i < hbm else x for i, x in enumerate(args))
    if not aliases:
        after = tuple(pltpu.with_memory_space_constraint(x, pltpu.HBM) for x in after)
    return pl.pallas_call(
        kernel,
        out_shape=out_shape,
        in_specs=placed(pltpu.HBM, hbm) + placed(pltpu.VMEM, len(args) - hbm) + placed(pl.ANY if aliases else pltpu.HBM, len(after)),
        out_specs=placed(out_space, len(out_shape)),
        input_output_aliases=aliases or {},
        scratch_shapes=list(scratch) + [pltpu.SemaphoreType.DMA(n if isinstance(n, tuple) else (n,)) for n in sems],
        compiler_params=pltpu.CompilerParams(vmem_limit_bytes=mega * 2**20),
        cost_estimate=pl.CostEstimate(flops=flops, bytes_accessed=moved, transcendentals=0),
        name=kernel.__name__,
    )(*args, *after)


def shift_z(step):
    return [(2 * z + x, 2 * ((z + step) % 4) + x) for z in range(4) for x in range(2)]


SWAP_X = [(2 * z + x, 2 * z + 1 - x) for z in range(4) for x in range(2)]


def exchange(values, axis):
    return lax.all_to_all(values, axis, split_axis=0, concat_axis=0, tiled=True)


def shifted(part, step):
    return lax.ppermute(part, "dp", shift_z(step))


def added(*parts):
    sums = parts[0].astype(F32)
    for part in parts[1:]:
        sums = sums + part.astype(F32)
    return sums.astype(BF)


def z_sums(f, s):
    f_on = shifted(f[2], 1)
    s_on = shifted(s[2], 3)
    s_got = shifted(s[1], 1)
    f_got = shifted(f[3], 3)
    f_far = shifted(added(f[1], f_on), 1)
    s_far = shifted(added(s[3], s_on), 3)
    (part,) = run(join, (f[0], f_got, f_far, s[0], s_got, s_far), (like(256, 1024),), 16, flops=1, moved=2 * 10**6)
    return part


def per_device(tokens, first_up, second_up, first_down, second_down, perm_up, perm_down, cotangent):
    perms = (perm_up.reshape(64, 128), perm_down.reshape(64, 128))
    square = near(512, 512)
    (sent,) = run(
        stage_one,
        (tokens, cotangent, first_up, second_down) + perms,
        (far(16, 64, 1024),),
        20,
        hbm=6,
        out_space=pltpu.HBM,
        scratch=[near(1024, 512)] * 2
        + [near(2, 256, 256)] * 2
        + [pltpu.VMEM((64, 128), jnp.int32)] * 2
        + [near(2, 512, 512)] * 2
        + [near(16, 64, 1024)],
        sems=(6, 4),
        flops=2 * 10**9,
        moved=5 * 10**6,
    )
    got = exchange(sent, "chan")
    up_src, up_tgt, down_src, down_tgt, w_up, w_down = run(
        prepare,
        (first_up, second_down) + perms,
        (far(512, 512), square) + (far(512, 512),) * 4,
        20,
        after=(sent,),
        flops=2 * 10**9,
        moved=4 * 10**6,
    )
    sent, *grads = run(
        stage_two,
        (down_src, second_up, first_down, pltpu.with_memory_space_constraint(up_tgt, pltpu.VMEM), got),
        (far(16, 64, 1024),) + (far(128, 1024),) * 8,
        32,
        hbm=3,
        out_space=pltpu.HBM,
        scratch=[square, near(2, 256, 1024), near(2, 1024, 256)]
        + [near(2, 1024, 1024)] * 2
        + [near(512, 1024)] * 2
        + [near(4, 128, 1024)] * 2
        + [near(16, 64, 1024)],
        sems=(3, 16),
        flops=85 * 10**8,
        moved=9 * 10**6,
    )
    got = exchange(sent, "chan")
    part = z_sums(grads[:4], grads[4:])
    other = lax.ppermute(part, "dp", SWAP_X)
    (chunk,) = run(pair, (part, other), (like(256, 1024),), 16, flops=1, moved=2 * 10**6)
    left, right = shifted(chunk, 1), shifted(chunk, 3)
    f_on, s_on = run(halves, (left, right), (like(128, 1024),) * 2, 16, flops=1, moved=10**6)
    f_far, s_far = shifted(f_on, 1), shifted(s_on, 3)
    (tail,) = run(
        square_grads,
        (tokens, cotangent, up_src, down_tgt, got),
        (far(8, 64, 512),),
        20,
        hbm=4,
        out_space=pltpu.HBM,
        scratch=[near(1024, 512)] * 2 + [square, square, near(8, 64, 512)],
        sems=(6, 2),
        flops=16 * 10**8,
        moved=5 * 10**6,
    )
    tail_parts = exchange(tail, "dp")
    mixed, input_grad = run(
        outputs,
        (w_up, w_down, got),
        (like(1024, 512),) * 2,
        20,
        hbm=2,
        after=(tail,),
        scratch=[square, square],
        sems=(2,),
        flops=10**9,
        moved=5 * 10**6,
    )
    (tail_sums,) = run(
        total, (tail_parts,), (far(8, 64, 512),), 20, after=(mixed,), flops=10**6, moved=10**6
    )
    tail_all = exchange(tail_sums, "dp")
    wide = (like(2, 1024, 256, dtype=F32), like(2, 256, 1024, dtype=F32))
    held = run(
        place_near,
        (chunk, left, right),
        wide,
        24,
        out_space=pl.ANY,
        scratch=[pltpu.VMEM((3, 512, 256), F32), pltpu.VMEM((3, 128, 1024), F32)],
        sems=((3, 2),),
        flops=10**6,
        moved=5 * 10**6,
    )
    small = like(2, 256, 256, dtype=F32)
    grad_fd, grad_su, grad_fu, grad_sd = run(
        finish,
        (f_far, s_far, tail_all),
        wide + (small, small),
        24,
        after=tuple(held),
        out_space=pl.ANY,
        aliases={3: 0, 4: 1},
        scratch=[pltpu.VMEM((512, 256), F32), pltpu.VMEM((128, 1024), F32)] + [pltpu.VMEM((2, 256, 256), F32)] * 2,
        sems=((2,), (2,)),
        flops=10**6,
        moved=4 * 10**6,
    )
    return (mixed, input_grad, grad_fu, grad_su, grad_fd, grad_sd)


def solution(mesh):
    layout = (
        P("dp", "chan"),
        P("chan", None, None),
        P("chan", None, None),
        P("chan", None, None),
        P("chan", None, None),
        P(),
        P(),
        P("dp", "chan"),
    )
    return jax.shard_map(
        per_device,
        mesh=mesh,
        in_specs=layout,
        out_specs=(
            P("dp", "chan"),
            P("dp", "chan"),
            P("chan", None, None),
            P("chan", None, None),
            P("chan", None, None),
            P("chan", None, None),
        ),
        check_vma=False,
    )
```

```python
import jax
import jax.numpy as jnp
from jax import lax
from jax.experimental import pallas as pl
from jax.experimental.pallas import tpu as pltpu
from jax.sharding import PartitionSpec as P

BF = jnp.bfloat16
F32 = jnp.float32
GELU_C = 0.7978845608028654
GELU_A = 0.044715


def nn(left, right):
    return lax.dot_general(left, right, (((1,), (0,)), ((), ())), preferred_element_type=F32)


def nt(left, right):
    return lax.dot_general(left, right, (((1,), (1,)), ((), ())), preferred_element_type=F32)


def tn(left, right):
    return lax.dot_general(left, right, (((0,), (0,)), ((), ())), preferred_element_type=F32)


def slot_order(perm_ref, me):
    rows, mine = [], []
    for i in range(4):
        rows.append(perm_ref[pl.ds(i, 16, stride=4), :])
        mine.append(perm_ref[pl.ds(4 * me + i, 1), :])
    perm = jnp.concatenate(rows, axis=1)
    own = jnp.concatenate(mine, axis=1)
    from_here = lax.shift_right_logical(perm, 9) == me
    from_group = lax.shift_right_logical(own, 9) == lax.broadcasted_iota(jnp.int32, (16, 512), 0)
    return from_here, (perm & 511).astype(F32), from_group


def ranks(hits):
    before = jnp.where(
        lax.broadcasted_iota(jnp.int32, (512, 512), 0) < lax.broadcasted_iota(jnp.int32, (512, 512), 1), 1.0, 0.0
    ).astype(BF)
    return jnp.where(hits, nn(jnp.where(hits, 1.0, 0.0).astype(BF), before), -1.0)


def source_matrix(perm_ref, me, ref):
    from_here, channel, _ = slot_order(perm_ref, me)
    rank = ranks(from_here)
    slot = lax.broadcasted_iota(jnp.int32, (32, 512), 0).astype(F32)
    lane = lax.broadcasted_iota(jnp.int32, (32, 512), 1).astype(F32)
    for r in range(16):
        hit = rank[r : r + 1, :] == slot
        source = jnp.sum(jnp.where(hit, channel[r : r + 1, :], 0.0), axis=1, keepdims=True)
        ref[32 * r : 32 * r + 32, :] = jnp.where(source == lane, 1.0, 0.0).astype(BF)


def target_matrix(perm_ref, me, ref):
    _, _, from_group = slot_order(perm_ref, me)
    rank = ranks(from_group)
    slot = lax.broadcasted_iota(jnp.int32, (32, 512), 0).astype(F32)
    for s in range(16):
        ref[32 * s : 32 * s + 32, :] = jnp.where(rank[s : s + 1, :] == slot, 1.0, 0.0).astype(BF)


def fold_up(source_ref, fu_ref, ref):
    for k in range(2):
        cols = slice(256 * k, 256 * k + 256)
        ref[:, cols] = nt(source_ref[:, cols], fu_ref[k]).astype(BF)


def fold_down(target_ref, sd_ref, ref):
    for k in range(2):
        cols = slice(256 * k, 256 * k + 256)
        ref[:, cols] = nn(target_ref[:, cols], sd_ref[k]).astype(BF)


def start(pairs, sems):
    copies = [pltpu.make_async_copy(source, target, sems.at[i]) for i, (source, target) in enumerate(pairs)]
    for copy in copies:
        copy.start()
    return copies


def send(source, target, sem):
    copy = pltpu.make_async_copy(source, target, sem)
    copy.start()
    return copy


def stage_one(
    tok_hbm, cot_hbm, fu_hbm, sd_hbm, pu_hbm, pd_hbm, out_hbm, tok, cot, fu, sd, pu, pd, matrix, weight, out, sems, out_sems
):
    copies = start(((pu_hbm, pu), (pd_hbm, pd), (fu_hbm, fu), (sd_hbm, sd), (tok_hbm, tok), (cot_hbm, cot)), sems)
    me = lax.axis_index("chan")
    copies[0].wait()
    copies[1].wait()
    copies[2].wait()
    copies[3].wait()
    source_matrix(pu, me, matrix.at[0])
    target_matrix(pd, me, matrix.at[1])
    fold_up(matrix.at[0], fu, weight.at[0])
    fold_down(matrix.at[1], sd, weight.at[1])
    sent = []
    copies[4].wait()
    copies[5].wait()
    for n, (i, groups) in enumerate(((0, slice(0, 16)), (1, slice(0, 8)), (1, slice(8, 16)))):
        slots = slice(32 * groups.start, 32 * groups.stop)
        part = nt(weight[i, slots, :], (tok, cot)[i][...]).astype(BF)
        out[groups, 32 * i : 32 * i + 32, :] = part.reshape(-1, 32, 1024)
        at = (groups, slice(32 * i, 32 * i + 32))
        sent.append(send(out.at[at], out_hbm.at[at], out_sems.at[n]))
    for copy in sent:
        copy.wait()


def prepare(fu_ref, sd_ref, pu_ref, pd_ref, mark, up_src, up_tgt, down_src, down_tgt, w_up, w_down):
    me = lax.axis_index("chan")
    source_matrix(pu_ref, me, up_src)
    target_matrix(pu_ref, me, up_tgt)
    source_matrix(pd_ref, me, down_src)
    target_matrix(pd_ref, me, down_tgt)
    fold_up(up_src, fu_ref, w_up)
    fold_down(down_tgt, sd_ref, w_down)


def stage_two(
    src_hbm, su_hbm, fd_hbm, up_tgt, r_ref, out_hbm, f0, f1, f2, f3, s0, s1, s2, s3,
    down_src, su, fd, act, hg, nar, mix, pfd, psu, out, sems, out_sems,
):
    copies = start(((src_hbm, down_src), (su_hbm, su), (fd_hbm, fd)), sems)
    mixed_in = tn(up_tgt[...], r_ref[:, 0:32, :].reshape(512, 1024)).astype(BF)
    copies[0].wait()
    nar_grad = tn(down_src[...], r_ref[:, 32:64, :].reshape(512, 1024)).astype(BF)
    copies[1].wait()
    copies[2].wait()
    z = lax.shift_right_logical(lax.axis_index("dp"), 1)
    sent = []
    size = 512
    steps = [(k, slice(size * c, size * c + size)) for k in range(2) for c in range(1024 // size)]

    def products(k, units):
        rows = slice(256 * k, 256 * k + 256)
        return tn(su[k, :, units], mixed_in[rows, :]), nn(fd[k, units, :], nar_grad[rows, :])

    ready = products(*steps[0])
    for n, (k, units) in enumerate(steps):
        v, up = ready
        if n + 1 < len(steps):
            ready = products(*steps[n + 1])
        sq = v * v
        h = 0.5 + 0.5 * jnp.tanh(v * (GELU_C + (GELU_C * GELU_A) * sq))
        a = (v * h).astype(BF)
        d = v * ((2 * GELU_C) + (6 * GELU_C * GELU_A) * sq)
        b = (up * (h * (1.0 + (1.0 - h) * d))).astype(BF)
        act[k, units, :] = a
        hg[k, units, :] = b
        gsu = nt(mixed_in[256 * k : 256 * k + 256, :], b).astype(BF)
        gfd = nt(a, nar_grad[256 * k : 256 * k + 256, :]).astype(BF)
        for i in range(2):
            psu[2 * k + i, :, units] = gsu[128 * i : 128 * i + 128, :]
        for i in range(size // 128):
            at = units.start + 128 * i
            lanes = slice(256 * ((at % 512) // 128), 256 * ((at % 512) // 128) + 256)
            pfd[2 * k + at // 512, :, lanes] = gfd[128 * i : 128 * i + 128, :]
        if units.stop == 1024:
            if k == 1:
                for i, (f, s) in enumerate(((f0, s0), (f1, s1), (f2, s2), (f3, s3))):
                    sent.append(send(pfd.at[(z + i) & 3], f, out_sems.at[i]))
                    sent.append(send(psu.at[(z + i) & 3], s, out_sems.at[4 + i]))
            nar[256 * k : 256 * k + 256, :] = tn(fd[k], act[k]).astype(BF)
            mix[256 * k : 256 * k + 256, :] = nn(su[k], hg[k]).astype(BF)
    for i, (matrix, rows) in enumerate(((down_src, nar), (up_tgt, mix))):
        for j in range(4):
            groups = slice(4 * j, 4 * j + 4)
            part = nn(matrix[128 * j : 128 * j + 128, :], rows[...]).astype(BF)
            out[groups, 32 * i : 32 * i + 32, :] = part.reshape(4, 32, 1024)
            at = (groups, slice(32 * i, 32 * i + 32))
            sent.append(send(out.at[at], out_hbm.at[at], out_sems.at[8 + 4 * i + j]))
    for copy in sent:
        copy.wait()


def square_grads(
    tok_hbm, cot_hbm, src_hbm, tgt_hbm, r_ref, t_hbm, tok, cot, up_src, down_tgt, t, sems, out_sems
):
    copies = start(((cot_hbm, cot), (tgt_hbm, down_tgt), (tok_hbm, tok), (src_hbm, up_src)), sems)
    sent = []
    for n, rows in enumerate((cot, tok)):
        copies[2 * n].wait()
        copies[2 * n + 1].wait()
        sums = nn(r_ref[:, 32 * n : 32 * n + 32, :].reshape(512, 1024), rows[...]).astype(BF)
        for k in range(2):
            cols = slice(256 * k, 256 * k + 256)
            grad = tn(down_tgt[:, cols], sums[:, cols]) if n == 0 else tn(sums[:, cols], up_src[:, cols])
            grad = grad.astype(BF)
            for i in range(4):
                t[4 * k + i, :, 256 * n : 256 * n + 256] = grad[64 * i : 64 * i + 64, :]
        at = (slice(0, 8), slice(0, 64), slice(256 * n, 256 * n + 256))
        sent.append(send(t.at[at], t_hbm.at[at], out_sems.at[n]))
    for copy in sent:
        copy.wait()


def outputs(up_hbm, down_hbm, r_ref, after, mixed_ref, ig_ref, w_up, w_down, sems):
    copies = start(((down_hbm, w_down), (up_hbm, w_up)), sems)
    copies[0].wait()
    mixed_ref[...] = tn(r_ref[:, 0:32, :].reshape(512, 1024), w_down[...]).astype(BF)
    copies[1].wait()
    ig_ref[...] = tn(r_ref[:, 32:64, :].reshape(512, 1024), w_up[...]).astype(BF)


def total(t_ref, after, out_ref):
    sums = t_ref[0].astype(F32)
    for i in range(1, 8):
        sums = sums + t_ref[i].astype(F32)
    sums = sums.astype(BF)
    for i in range(8):
        out_ref[i] = sums


def join(f0, f1, f2, s0, s1, s2, out_ref):
    out_ref[0:128, :] = (f0[...].astype(F32) + f1[...].astype(F32) + f2[...].astype(F32)).astype(BF)
    out_ref[128:256, :] = (s0[...].astype(F32) + s1[...].astype(F32) + s2[...].astype(F32)).astype(BF)


def pair(mine, other, out_ref):
    out_ref[...] = (mine[...].astype(F32) + other[...].astype(F32)).astype(BF)


def halves(left, right, f_out, s_out):
    f_out[...] = left[0:128, :]
    s_out[...] = right[128:256, :]


def place(part_f, part_s, step, fd, su, fd_hbm, su_hbm, sems):
    for b in range(4):
        fd[128 * b : 128 * b + 128, :] = part_f[:, 256 * b : 256 * b + 256].astype(F32)
    su[...] = part_s[...].astype(F32)
    c = (lax.shift_right_logical(lax.axis_index("dp"), 1) - step) & 3
    fd_at = fd_hbm.at[c >> 1, pl.ds(pl.multiple_of((c & 1) * 512, 512), 512)]
    su_at = su_hbm.at[c >> 1, pl.ds(pl.multiple_of((c & 1) * 128, 128), 128)]
    return start(((fd, fd_at), (su, su_at)), sems)


def place_near(own, left, right, fd_hbm, su_hbm, fd, su, sems):
    sent = []
    for n, (part, step) in enumerate(((own, 0), (left, 1), (right, 3))):
        halves = (part.at[0:128], part.at[128:256])
        sent += place(*halves, step, fd.at[n], su.at[n], fd_hbm, su_hbm, sems.at[n])
    for copy in sent:
        copy.wait()


def finish(f_far, s_far, t_ref, fd_in, su_in, fd_hbm, su_hbm, gfu_hbm, gsd_hbm, fd, su, gfu, gsd, sems, more_sems):
    sent = place(f_far, s_far, 2, fd, su, fd_hbm, su_hbm, sems)
    for k in range(2):
        for i in range(4):
            rows = slice(64 * i, 64 * i + 64)
            gsd[k, rows, :] = t_ref[4 * k + i, :, 0:256].astype(F32)
            gfu[k, rows, :] = t_ref[4 * k + i, :, 256:512].astype(F32)
    sent += start(((gfu, gfu_hbm), (gsd, gsd_hbm)), more_sems)
    for copy in sent:
        copy.wait()


def like(*shape, dtype=BF):
    return jax.ShapeDtypeStruct(shape, dtype)


def far(*shape):
    return pltpu.HBM(shape, BF)


def near(*shape):
    return pltpu.VMEM(shape, BF)


def placed(space, count):
    return [pl.BlockSpec(memory_space=space)] * count


def run(kernel, args, out_shape, mega, hbm=0, after=(), out_space=pltpu.VMEM, aliases=None, scratch=(), sems=(), flops=0, moved=0):
    args = tuple(pltpu.with_memory_space_constraint(x, pltpu.HBM) if i < hbm else x for i, x in enumerate(args))
    if not aliases:
        after = tuple(pltpu.with_memory_space_constraint(x, pltpu.HBM) for x in after)
    return pl.pallas_call(
        kernel,
        out_shape=out_shape,
        in_specs=placed(pltpu.HBM, hbm) + placed(pltpu.VMEM, len(args) - hbm) + placed(pl.ANY if aliases else pltpu.HBM, len(after)),
        out_specs=placed(out_space, len(out_shape)),
        input_output_aliases=aliases or {},
        scratch_shapes=list(scratch) + [pltpu.SemaphoreType.DMA(n if isinstance(n, tuple) else (n,)) for n in sems],
        compiler_params=pltpu.CompilerParams(vmem_limit_bytes=mega * 2**20),
        cost_estimate=pl.CostEstimate(flops=flops, bytes_accessed=moved, transcendentals=0),
        name=kernel.__name__,
    )(*args, *after)


def shift_z(step):
    return [(2 * z + x, 2 * ((z + step) % 4) + x) for z in range(4) for x in range(2)]


SWAP_X = [(2 * z + x, 2 * z + 1 - x) for z in range(4) for x in range(2)]


def exchange(values, axis):
    return lax.all_to_all(values, axis, split_axis=0, concat_axis=0, tiled=True)


def shifted(part, step):
    return lax.ppermute(part, "dp", shift_z(step))


def added(*parts):
    sums = parts[0].astype(F32)
    for part in parts[1:]:
        sums = sums + part.astype(F32)
    return sums.astype(BF)


def z_sums(f, s):
    f_on = shifted(f[2], 1)
    s_on = shifted(s[2], 3)
    s_got = shifted(s[1], 1)
    f_got = shifted(f[3], 3)
    f_far = shifted(added(f[1], f_on), 1)
    s_far = shifted(added(s[3], s_on), 3)
    (part,) = run(join, (f[0], f_got, f_far, s[0], s_got, s_far), (like(256, 1024),), 16, flops=1, moved=2 * 10**6)
    return part


def per_device(tokens, first_up, second_up, first_down, second_down, perm_up, perm_down, cotangent):
    perms = (perm_up.reshape(64, 128), perm_down.reshape(64, 128))
    square = near(512, 512)
    (sent,) = run(
        stage_one,
        (tokens, cotangent, first_up, second_down) + perms,
        (far(16, 64, 1024),),
        20,
        hbm=6,
        out_space=pltpu.HBM,
        scratch=[near(1024, 512)] * 2
        + [near(2, 256, 256)] * 2
        + [pltpu.VMEM((64, 128), jnp.int32)] * 2
        + [near(2, 512, 512)] * 2
        + [near(16, 64, 1024)],
        sems=(6, 4),
        flops=2 * 10**9,
        moved=5 * 10**6,
    )
    got = exchange(sent, "chan")
    up_src, up_tgt, down_src, down_tgt, w_up, w_down = run(
        prepare,
        (first_up, second_down) + perms,
        (far(512, 512), square) + (far(512, 512),) * 4,
        20,
        after=(sent,),
        flops=2 * 10**9,
        moved=4 * 10**6,
    )
    sent, *grads = run(
        stage_two,
        (down_src, second_up, first_down, pltpu.with_memory_space_constraint(up_tgt, pltpu.VMEM), got),
        (far(16, 64, 1024),) + (far(128, 1024),) * 8,
        32,
        hbm=3,
        out_space=pltpu.HBM,
        scratch=[square, near(2, 256, 1024), near(2, 1024, 256)]
        + [near(2, 1024, 1024)] * 2
        + [near(512, 1024)] * 2
        + [near(4, 128, 1024)] * 2
        + [near(16, 64, 1024)],
        sems=(3, 16),
        flops=85 * 10**8,
        moved=9 * 10**6,
    )
    got = exchange(sent, "chan")
    part = z_sums(grads[:4], grads[4:])
    other = lax.ppermute(part, "dp", SWAP_X)
    (chunk,) = run(pair, (part, other), (like(256, 1024),), 16, flops=1, moved=2 * 10**6)
    left, right = shifted(chunk, 1), shifted(chunk, 3)
    f_on, s_on = run(halves, (left, right), (like(128, 1024),) * 2, 16, flops=1, moved=10**6)
    f_far, s_far = shifted(f_on, 1), shifted(s_on, 3)
    (tail,) = run(
        square_grads,
        (tokens, cotangent, up_src, down_tgt, got),
        (far(8, 64, 512),),
        20,
        hbm=4,
        out_space=pltpu.HBM,
        scratch=[near(1024, 512)] * 2 + [square, square, near(8, 64, 512)],
        sems=(6, 2),
        flops=16 * 10**8,
        moved=5 * 10**6,
    )
    tail_parts = exchange(tail, "dp")
    mixed, input_grad = run(
        outputs,
        (w_up, w_down, got),
        (like(1024, 512),) * 2,
        20,
        hbm=2,
        after=(tail,),
        scratch=[square, square],
        sems=(2,),
        flops=10**9,
        moved=5 * 10**6,
    )
    (tail_sums,) = run(
        total, (tail_parts,), (far(8, 64, 512),), 20, after=(mixed,), flops=10**6, moved=10**6
    )
    tail_all = exchange(tail_sums, "dp")
    wide = (like(2, 1024, 256, dtype=F32), like(2, 256, 1024, dtype=F32))
    held = run(
        place_near,
        (chunk, left, right),
        wide,
        24,
        out_space=pl.ANY,
        scratch=[pltpu.VMEM((3, 512, 256), F32), pltpu.VMEM((3, 128, 1024), F32)],
        sems=((3, 2),),
        flops=10**6,
        moved=5 * 10**6,
    )
    small = like(2, 256, 256, dtype=F32)
    grad_fd, grad_su, grad_fu, grad_sd = run(
        finish,
        (f_far, s_far, tail_all),
        wide + (small, small),
        24,
        after=tuple(held),
        out_space=pl.ANY,
        aliases={3: 0, 4: 1},
        scratch=[pltpu.VMEM((512, 256), F32), pltpu.VMEM((128, 1024), F32)] + [pltpu.VMEM((2, 256, 256), F32)] * 2,
        sems=((2,), (2,)),
        flops=10**6,
        moved=4 * 10**6,
    )
    return (mixed, input_grad, grad_fu, grad_su, grad_fd, grad_sd)


def solution(mesh):
    layout = (
        P("dp", "chan"),
        P("chan", None, None),
        P("chan", None, None),
        P("chan", None, None),
        P("chan", None, None),
        P(),
        P(),
        P("dp", "chan"),
    )
    return jax.shard_map(
        per_device,
        mesh=mesh,
        in_specs=layout,
        out_specs=(
            P("dp", "chan"),
            P("dp", "chan"),
            P("chan", None, None),
            P("chan", None, None),
            P("chan", None, None),
            P("chan", None, None),
        ),
        check_vma=False,
    )
```

```python
import jax
import jax.numpy as jnp
from jax import lax
from jax.experimental import pallas as pl
from jax.experimental.pallas import tpu as pltpu
from jax.sharding import PartitionSpec as P

BF = jnp.bfloat16
F32 = jnp.float32
GELU_C = 0.7978845608028654
GELU_A = 0.044715


def nn(left, right):
    return lax.dot_general(left, right, (((1,), (0,)), ((), ())), preferred_element_type=F32)


def nt(left, right):
    return lax.dot_general(left, right, (((1,), (1,)), ((), ())), preferred_element_type=F32)


def tn(left, right):
    return lax.dot_general(left, right, (((0,), (0,)), ((), ())), preferred_element_type=F32)


def slot_order(perm_ref, me):
    rows, mine = [], []
    for i in range(4):
        rows.append(perm_ref[pl.ds(i, 16, stride=4), :])
        mine.append(perm_ref[pl.ds(4 * me + i, 1), :])
    perm = jnp.concatenate(rows, axis=1)
    own = jnp.concatenate(mine, axis=1)
    from_here = lax.shift_right_logical(perm, 9) == me
    from_group = lax.shift_right_logical(own, 9) == lax.broadcasted_iota(jnp.int32, (16, 512), 0)
    return from_here, (perm & 511).astype(F32), from_group


def ranks(hits):
    before = jnp.where(
        lax.broadcasted_iota(jnp.int32, (512, 512), 0) < lax.broadcasted_iota(jnp.int32, (512, 512), 1), 1.0, 0.0
    ).astype(BF)
    return jnp.where(hits, nn(jnp.where(hits, 1.0, 0.0).astype(BF), before), -1.0)


def source_matrix(perm_ref, me, ref):
    from_here, channel, _ = slot_order(perm_ref, me)
    rank = ranks(from_here)
    slot = lax.broadcasted_iota(jnp.int32, (32, 512), 0).astype(F32)
    lane = lax.broadcasted_iota(jnp.int32, (32, 512), 1).astype(F32)
    for r in range(16):
        hit = rank[r : r + 1, :] == slot
        source = jnp.sum(jnp.where(hit, channel[r : r + 1, :], 0.0), axis=1, keepdims=True)
        ref[32 * r : 32 * r + 32, :] = jnp.where(source == lane, 1.0, 0.0).astype(BF)


def target_matrix(perm_ref, me, ref):
    _, _, from_group = slot_order(perm_ref, me)
    rank = ranks(from_group)
    slot = lax.broadcasted_iota(jnp.int32, (32, 512), 0).astype(F32)
    for s in range(16):
        ref[32 * s : 32 * s + 32, :] = jnp.where(rank[s : s + 1, :] == slot, 1.0, 0.0).astype(BF)


def fold_up(source_ref, fu_ref, ref):
    for k in range(2):
        cols = slice(256 * k, 256 * k + 256)
        ref[:, cols] = nt(source_ref[:, cols], fu_ref[k]).astype(BF)


def fold_down(target_ref, sd_ref, ref):
    for k in range(2):
        cols = slice(256 * k, 256 * k + 256)
        ref[:, cols] = nn(target_ref[:, cols], sd_ref[k]).astype(BF)


def start(pairs, sems):
    copies = [pltpu.make_async_copy(source, target, sems.at[i]) for i, (source, target) in enumerate(pairs)]
    for copy in copies:
        copy.start()
    return copies


def send(source, target, sem):
    copy = pltpu.make_async_copy(source, target, sem)
    copy.start()
    return copy


def stage_one(
    tok_hbm, cot_hbm, fu_hbm, sd_hbm, pu_hbm, pd_hbm, out_hbm, tok, cot, fu, sd, pu, pd, matrix, weight, out, sems, out_sems
):
    copies = start(((pu_hbm, pu), (pd_hbm, pd), (fu_hbm, fu), (sd_hbm, sd), (tok_hbm, tok), (cot_hbm, cot)), sems)
    me = lax.axis_index("chan")
    copies[0].wait()
    copies[1].wait()
    copies[2].wait()
    copies[3].wait()
    source_matrix(pu, me, matrix.at[0])
    target_matrix(pd, me, matrix.at[1])
    fold_up(matrix.at[0], fu, weight.at[0])
    fold_down(matrix.at[1], sd, weight.at[1])
    sent = []
    copies[4].wait()
    copies[5].wait()
    for n, (i, groups) in enumerate(((0, slice(0, 16)), (1, slice(0, 8)), (1, slice(8, 16)))):
        slots = slice(32 * groups.start, 32 * groups.stop)
        part = nt(weight[i, slots, :], (tok, cot)[i][...]).astype(BF)
        out[groups, 32 * i : 32 * i + 32, :] = part.reshape(-1, 32, 1024)
        at = (groups, slice(32 * i, 32 * i + 32))
        sent.append(send(out.at[at], out_hbm.at[at], out_sems.at[n]))
    for copy in sent:
        copy.wait()


def prepare(fu_ref, sd_ref, pu_ref, pd_ref, mark, up_src, up_tgt, down_src, down_tgt, w_up, w_down):
    me = lax.axis_index("chan")
    source_matrix(pu_ref, me, up_src)
    target_matrix(pu_ref, me, up_tgt)
    source_matrix(pd_ref, me, down_src)
    target_matrix(pd_ref, me, down_tgt)
    fold_up(up_src, fu_ref, w_up)
    fold_down(down_tgt, sd_ref, w_down)


def stage_two(
    src_hbm, su_hbm, fd_hbm, up_tgt, r_ref, out_hbm, f0, f1, f2, f3, s0, s1, s2, s3,
    down_src, su, fd, act, hg, nar, mix, pfd, psu, out, sems, out_sems,
):
    copies = start(((src_hbm, down_src), (su_hbm, su), (fd_hbm, fd)), sems)
    mixed_in = tn(up_tgt[...], r_ref[:, 0:32, :].reshape(512, 1024)).astype(BF)
    copies[0].wait()
    nar_grad = tn(down_src[...], r_ref[:, 32:64, :].reshape(512, 1024)).astype(BF)
    copies[1].wait()
    copies[2].wait()
    z = lax.shift_right_logical(lax.axis_index("dp"), 1)
    sent = []
    size = 512
    steps = [(k, slice(size * c, size * c + size)) for k in range(2) for c in range(1024 // size)]

    def products(k, units):
        rows = slice(256 * k, 256 * k + 256)
        return tn(su[k, :, units], mixed_in[rows, :]), nn(fd[k, units, :], nar_grad[rows, :])

    ready = products(*steps[0])
    for n, (k, units) in enumerate(steps):
        v, up = ready
        if n + 1 < len(steps):
            ready = products(*steps[n + 1])
        sq = v * v
        h = 0.5 + 0.5 * jnp.tanh(v * (GELU_C + (GELU_C * GELU_A) * sq))
        a = (v * h).astype(BF)
        d = v * ((2 * GELU_C) + (6 * GELU_C * GELU_A) * sq)
        b = (up * (h * (1.0 + (1.0 - h) * d))).astype(BF)
        act[k, units, :] = a
        hg[k, units, :] = b
        gsu = nt(mixed_in[256 * k : 256 * k + 256, :], b).astype(BF)
        gfd = nt(a, nar_grad[256 * k : 256 * k + 256, :]).astype(BF)
        for i in range(2):
            psu[2 * k + i, :, units] = gsu[128 * i : 128 * i + 128, :]
        for i in range(size // 128):
            at = units.start + 128 * i
            lanes = slice(256 * ((at % 512) // 128), 256 * ((at % 512) // 128) + 256)
            pfd[2 * k + at // 512, :, lanes] = gfd[128 * i : 128 * i + 128, :]
        if units.stop == 1024:
            if k == 1:
                for i, (f, s) in enumerate(((f0, s0), (f1, s1), (f2, s2), (f3, s3))):
                    sent.append(send(pfd.at[(z + i) & 3], f, out_sems.at[i]))
                    sent.append(send(psu.at[(z + i) & 3], s, out_sems.at[4 + i]))
            nar[256 * k : 256 * k + 256, :] = tn(fd[k], act[k]).astype(BF)
            mix[256 * k : 256 * k + 256, :] = nn(su[k], hg[k]).astype(BF)
    for i, (matrix, rows) in enumerate(((down_src, nar), (up_tgt, mix))):
        for j in range(4):
            groups = slice(4 * j, 4 * j + 4)
            part = nn(matrix[128 * j : 128 * j + 128, :], rows[...]).astype(BF)
            out[groups, 32 * i : 32 * i + 32, :] = part.reshape(4, 32, 1024)
            at = (groups, slice(32 * i, 32 * i + 32))
            sent.append(send(out.at[at], out_hbm.at[at], out_sems.at[8 + 4 * i + j]))
    for copy in sent:
        copy.wait()


def square_grads(
    tok_hbm, cot_hbm, src_hbm, tgt_hbm, r_ref, t_hbm, tok, cot, up_src, down_tgt, t, sems, out_sems
):
    copies = start(((cot_hbm, cot), (tgt_hbm, down_tgt), (tok_hbm, tok), (src_hbm, up_src)), sems)
    sent = []
    for n, rows in enumerate((cot, tok)):
        copies[2 * n].wait()
        copies[2 * n + 1].wait()
        sums = nn(r_ref[:, 32 * n : 32 * n + 32, :].reshape(512, 1024), rows[...]).astype(BF)
        for k in range(2):
            cols = slice(256 * k, 256 * k + 256)
            grad = tn(down_tgt[:, cols], sums[:, cols]) if n == 0 else tn(sums[:, cols], up_src[:, cols])
            grad = grad.astype(BF)
            for i in range(4):
                t[4 * k + i, :, 256 * n : 256 * n + 256] = grad[64 * i : 64 * i + 64, :]
        at = (slice(0, 8), slice(0, 64), slice(256 * n, 256 * n + 256))
        sent.append(send(t.at[at], t_hbm.at[at], out_sems.at[n]))
    for copy in sent:
        copy.wait()


def outputs(up_hbm, down_hbm, r_ref, after, mixed_ref, ig_ref, w_up, w_down, sems):
    copies = start(((down_hbm, w_down), (up_hbm, w_up)), sems)
    copies[0].wait()
    mixed_ref[...] = tn(r_ref[:, 0:32, :].reshape(512, 1024), w_down[...]).astype(BF)
    copies[1].wait()
    ig_ref[...] = tn(r_ref[:, 32:64, :].reshape(512, 1024), w_up[...]).astype(BF)


def total(t_ref, out_ref):
    sums = t_ref[0].astype(F32)
    for i in range(1, 8):
        sums = sums + t_ref[i].astype(F32)
    sums = sums.astype(BF)
    for i in range(8):
        out_ref[i] = sums


def join(f0, f1, f2, s0, s1, s2, out_ref):
    out_ref[0:128, :] = (f0[...].astype(F32) + f1[...].astype(F32) + f2[...].astype(F32)).astype(BF)
    out_ref[128:256, :] = (s0[...].astype(F32) + s1[...].astype(F32) + s2[...].astype(F32)).astype(BF)


def pair(mine, other, out_ref):
    out_ref[...] = (mine[...].astype(F32) + other[...].astype(F32)).astype(BF)


def halves(left, right, f_out, s_out):
    f_out[...] = left[0:128, :]
    s_out[...] = right[128:256, :]


def place(part_f, part_s, step, fd, su, fd_hbm, su_hbm, sems):
    for b in range(4):
        fd[128 * b : 128 * b + 128, :] = part_f[:, 256 * b : 256 * b + 256].astype(F32)
    su[...] = part_s[...].astype(F32)
    c = (lax.shift_right_logical(lax.axis_index("dp"), 1) - step) & 3
    fd_at = fd_hbm.at[c >> 1, pl.ds(pl.multiple_of((c & 1) * 512, 512), 512)]
    su_at = su_hbm.at[c >> 1, pl.ds(pl.multiple_of((c & 1) * 128, 128), 128)]
    return start(((fd, fd_at), (su, su_at)), sems)


def place_near(own, left, right, fd_hbm, su_hbm, fd, su, sems):
    sent = []
    for n, (part, step) in enumerate(((own, 0), (left, 1), (right, 3))):
        halves = (part.at[0:128], part.at[128:256])
        sent += place(*halves, step, fd.at[n], su.at[n], fd_hbm, su_hbm, sems.at[n])
    for copy in sent:
        copy.wait()


def finish(f_far, s_far, t_ref, fd_in, su_in, fd_hbm, su_hbm, gfu_hbm, gsd_hbm, fd, su, gfu, gsd, sems, more_sems):
    sent = place(f_far, s_far, 2, fd, su, fd_hbm, su_hbm, sems)
    for k in range(2):
        for i in range(4):
            rows = slice(64 * i, 64 * i + 64)
            gsd[k, rows, :] = t_ref[4 * k + i, :, 0:256].astype(F32)
            gfu[k, rows, :] = t_ref[4 * k + i, :, 256:512].astype(F32)
    sent += start(((gfu, gfu_hbm), (gsd, gsd_hbm)), more_sems)
    for copy in sent:
        copy.wait()


def like(*shape, dtype=BF):
    return jax.ShapeDtypeStruct(shape, dtype)


def far(*shape):
    return pltpu.HBM(shape, BF)


def near(*shape):
    return pltpu.VMEM(shape, BF)


def placed(space, count):
    return [pl.BlockSpec(memory_space=space)] * count


def run(kernel, args, out_shape, mega, hbm=0, after=(), out_space=pltpu.VMEM, aliases=None, scratch=(), sems=(), flops=0, moved=0):
    args = tuple(pltpu.with_memory_space_constraint(x, pltpu.HBM) if i < hbm else x for i, x in enumerate(args))
    if not aliases:
        after = tuple(pltpu.with_memory_space_constraint(x, pltpu.HBM) for x in after)
    return pl.pallas_call(
        kernel,
        out_shape=out_shape,
        in_specs=placed(pltpu.HBM, hbm) + placed(pltpu.VMEM, len(args) - hbm) + placed(pl.ANY if aliases else pltpu.HBM, len(after)),
        out_specs=placed(out_space, len(out_shape)),
        input_output_aliases=aliases or {},
        scratch_shapes=list(scratch) + [pltpu.SemaphoreType.DMA(n if isinstance(n, tuple) else (n,)) for n in sems],
        compiler_params=pltpu.CompilerParams(vmem_limit_bytes=mega * 2**20),
        cost_estimate=pl.CostEstimate(flops=flops, bytes_accessed=moved, transcendentals=0),
        name=kernel.__name__,
    )(*args, *after)


def shift_z(step):
    return [(2 * z + x, 2 * ((z + step) % 4) + x) for z in range(4) for x in range(2)]


SWAP_X = [(2 * z + x, 2 * z + 1 - x) for z in range(4) for x in range(2)]


def exchange(values, axis):
    return lax.all_to_all(values, axis, split_axis=0, concat_axis=0, tiled=True)


def shifted(part, step):
    return lax.ppermute(part, "dp", shift_z(step))


def added(*parts):
    sums = parts[0].astype(F32)
    for part in parts[1:]:
        sums = sums + part.astype(F32)
    return sums.astype(BF)


def z_sums(f, s):
    f_on = shifted(f[2], 1)
    s_on = shifted(s[2], 3)
    s_got = shifted(s[1], 1)
    f_got = shifted(f[3], 3)
    f_far = shifted(added(f[1], f_on), 1)
    s_far = shifted(added(s[3], s_on), 3)
    (part,) = run(join, (f[0], f_got, f_far, s[0], s_got, s_far), (like(256, 1024),), 16, flops=1, moved=2 * 10**6)
    return part


def per_device(tokens, first_up, second_up, first_down, second_down, perm_up, perm_down, cotangent):
    perms = (perm_up.reshape(64, 128), perm_down.reshape(64, 128))
    square = near(512, 512)
    (sent,) = run(
        stage_one,
        (tokens, cotangent, first_up, second_down) + perms,
        (far(16, 64, 1024),),
        20,
        hbm=6,
        out_space=pltpu.HBM,
        scratch=[near(1024, 512)] * 2
        + [near(2, 256, 256)] * 2
        + [pltpu.VMEM((64, 128), jnp.int32)] * 2
        + [near(2, 512, 512)] * 2
        + [near(16, 64, 1024)],
        sems=(6, 4),
        flops=2 * 10**9,
        moved=5 * 10**6,
    )
    got = exchange(sent, "chan")
    up_src, up_tgt, down_src, down_tgt, w_up, w_down = run(
        prepare,
        (first_up, second_down) + perms,
        (far(512, 512), square) + (far(512, 512),) * 4,
        20,
        after=(sent,),
        flops=2 * 10**9,
        moved=4 * 10**6,
    )
    sent, *grads = run(
        stage_two,
        (down_src, second_up, first_down, pltpu.with_memory_space_constraint(up_tgt, pltpu.VMEM), got),
        (far(16, 64, 1024),) + (far(128, 1024),) * 8,
        32,
        hbm=3,
        out_space=pltpu.HBM,
        scratch=[square, near(2, 256, 1024), near(2, 1024, 256)]
        + [near(2, 1024, 1024)] * 2
        + [near(512, 1024)] * 2
        + [near(4, 128, 1024)] * 2
        + [near(16, 64, 1024)],
        sems=(3, 16),
        flops=85 * 10**8,
        moved=9 * 10**6,
    )
    got = exchange(sent, "chan")
    part = z_sums(grads[:4], grads[4:])
    other = lax.ppermute(part, "dp", SWAP_X)
    (chunk,) = run(pair, (part, other), (like(256, 1024),), 16, flops=1, moved=2 * 10**6)
    left, right = shifted(chunk, 1), shifted(chunk, 3)
    f_on, s_on = run(halves, (left, right), (like(128, 1024),) * 2, 16, flops=1, moved=10**6)
    f_far, s_far = shifted(f_on, 1), shifted(s_on, 3)
    (tail,) = run(
        square_grads,
        (tokens, cotangent, up_src, down_tgt, got),
        (far(8, 64, 512),),
        20,
        hbm=4,
        out_space=pltpu.HBM,
        scratch=[near(1024, 512)] * 2 + [square, square, near(8, 64, 512)],
        sems=(6, 2),
        flops=16 * 10**8,
        moved=5 * 10**6,
    )
    tail_parts = exchange(tail, "dp")
    (tail_sums,) = run(
        total, (tail_parts,), (far(8, 64, 512),), 20, flops=10**6, moved=10**6
    )
    mixed, input_grad = run(
        outputs,
        (w_up, w_down, got),
        (like(1024, 512),) * 2,
        20,
        hbm=2,
        after=(tail_sums,),
        scratch=[square, square],
        sems=(2,),
        flops=10**9,
        moved=5 * 10**6,
    )
    tail_all = exchange(tail_sums, "dp")
    wide = (like(2, 1024, 256, dtype=F32), like(2, 256, 1024, dtype=F32))
    held = run(
        place_near,
        (chunk, left, right),
        wide,
        24,
        out_space=pl.ANY,
        scratch=[pltpu.VMEM((3, 512, 256), F32), pltpu.VMEM((3, 128, 1024), F32)],
        sems=((3, 2),),
        flops=10**6,
        moved=5 * 10**6,
    )
    small = like(2, 256, 256, dtype=F32)
    grad_fd, grad_su, grad_fu, grad_sd = run(
        finish,
        (f_far, s_far, tail_all),
        wide + (small, small),
        24,
        after=tuple(held),
        out_space=pl.ANY,
        aliases={3: 0, 4: 1},
        scratch=[pltpu.VMEM((512, 256), F32), pltpu.VMEM((128, 1024), F32)] + [pltpu.VMEM((2, 256, 256), F32)] * 2,
        sems=((2,), (2,)),
        flops=10**6,
        moved=4 * 10**6,
    )
    return (mixed, input_grad, grad_fu, grad_su, grad_fd, grad_sd)


def solution(mesh):
    layout = (
        P("dp", "chan"),
        P("chan", None, None),
        P("chan", None, None),
        P("chan", None, None),
        P("chan", None, None),
        P(),
        P(),
        P("dp", "chan"),
    )
    return jax.shard_map(
        per_device,
        mesh=mesh,
        in_specs=layout,
        out_specs=(
            P("dp", "chan"),
            P("dp", "chan"),
            P("chan", None, None),
            P("chan", None, None),
            P("chan", None, None),
            P("chan", None, None),
        ),
        check_vma=False,
    )
```
